256 devices in a mesh: uly: 16 (over z_lo, y), blk: 16 (over z_hi, x, core).
Axes of the slice: x: 4, y: 4, z: 8 (z_hi: 2, z_lo: 4; z = z_hi * 4 + z_lo), core: 2. Of those that a mesh axis runs over, the one named last changes fastest.
Arguments:
- queries: bfloat16 [8192, 5120], P(('blk', 'uly')), may hold values from -60 to 60
- keys: bfloat16 [8192, 5120], P(('blk', 'uly')), may hold values from -9 to 9
- values: bfloat16 [8192, 5120], P(('blk', 'uly')), may hold values from -6 to 6
- row_counts: int32 [16], replicated, may hold values from 64 to 448, as said below
Outputs:
- attended: bfloat16 [8192, 4096], P(('blk', 'uly'))
- leftover_rows: bfloat16 [114688, 128], P(('blk', 'uly'))
The draws below stay inside these ranges and needn't reach their ends.
Inputs may be any that keep to these rules, and one draw needn't show every extreme that they name: `row_counts`: entry u counts the query rows of leftover head 32 + u // 2 that device u of each uly group serves; the 2 consecutive entries of one head sum to 512; some entry equals 448.
All inputs are finite; a program needn't handle non-finite values.
Results may differ from the reference program's by a relative error of at most 0.0095.
Values may be sent and summed in bfloat16 or wider, within the bound.
A program may use at most 64 MiB of HBM per device.

```python
import math
import jax
import jax.numpy as jnp
from jax import lax

HEADS = 40
HEAD_DIM = 128
MAIN = 32
LEFT = 8
PER = 2
GROUP = 512
SEQ = 8192
MOST = 448
N_ULY = 16
N_BLK = 16


def shared_field(key):
    return jnp.clip(jax.random.normal(key, (SEQ, HEADS * HEAD_DIM), jnp.float32), -4.0, 4.0)


def draw_keys(key, part):
    base_field = shared_field(key)
    result = base_field
    return result.astype(jnp.bfloat16)


def draw_queries(key, part):
    key = jax.random.fold_in(key, 7)
    result = jnp.clip(jax.random.normal(key, (SEQ, HEADS * HEAD_DIM), jnp.float32), -4.0, 4.0)
    return result.astype(jnp.bfloat16)


def draw_row_counts(key, part):
    key = jax.random.fold_in(key, 9)
    chosen = jax.random.randint(jax.random.fold_in(key, 2), (), 0, LEFT)
    if PER == 1:
        lowest = GROUP - GROUP // 8
        single = jax.random.randint(jax.random.fold_in(key, 4), (N_ULY,), lowest, GROUP + 1)
        single = jnp.where(jnp.arange(N_ULY) == chosen, MOST, single)
        return single.astype(jnp.int32)
    first_count = jax.random.randint(jax.random.fold_in(key, 1), (LEFT,), GROUP - MOST, MOST + 1)
    first_count = jnp.where(jnp.arange(LEFT) == chosen, MOST, first_count)
    flipped = jax.random.randint(jax.random.fold_in(key, 3), (LEFT,), 0, 2)
    first_count = jnp.where(flipped == 1, GROUP - first_count, first_count)
    paired = jnp.stack([first_count, GROUP - first_count], axis=1)
    return paired.reshape(N_ULY).astype(jnp.int32)


def steps_of(own_key, shape, pieces, least, largest):
    factor_of = 1.0
    for position, shards_of in pieces:
        steps = jax.random.uniform(jax.random.fold_in(jax.random.fold_in(own_key, 6), position), (shards_of,), jnp.float32, least / len(pieces), largest / len(pieces))
        factor_of = factor_of * jnp.repeat(jnp.exp(steps), shape[position] // shards_of).reshape((-1,) + (1,) * (len(shape) - 1 - position))
    return factor_of


def normal_values(rng, shape, width, bound, pieces=(), kind=jnp.bfloat16):
    drawn = jax.random.normal(rng, shape, jnp.float32) * width
    if len(pieces) > 0:
        drawn = steps_of(rng, shape, pieces, -0.22, 0.18) * drawn
    return jnp.clip(drawn, min=-bound, max=bound).astype(kind)


def setup_inputs(seed: int = 0) -> dict:
    streams_of = jax.random.split(jax.random.key(seed), 5)
    return {
        "queries": draw_queries(jax.random.fold_in(streams_of[4], 71), 0),
        "keys": draw_keys(jax.random.fold_in(streams_of[4], 71), 0),
        "values": normal_values(streams_of[2], (SEQ, HEADS * HEAD_DIM), 1.0, 6.0, ((0, 256),)),
        "row_counts": draw_row_counts(jax.random.fold_in(streams_of[4], 71), 0),
    }


def head_attention(query_head, key_head, value_head):
    score_scale = HEAD_DIM ** -0.5
    block_rows = math.gcd(SEQ, 512)

    def one_block(query_block):
        scores = jnp.dot(query_block, key_head.T, preferred_element_type=jnp.float32) * score_scale
        top = jnp.max(scores, axis=1, keepdims=True)
        weights = jnp.exp(scores - top)
        total = jnp.sum(weights, axis=1, keepdims=True)
        summed = jnp.dot(weights.astype(jnp.bfloat16), value_head, preferred_element_type=jnp.float32)
        return (summed / total).astype(jnp.bfloat16)

    blocks = query_head.reshape(SEQ // block_rows, block_rows, HEAD_DIM)
    return lax.map(one_block, blocks).reshape(SEQ, HEAD_DIM)


def reference(queries, keys, values, row_counts):
    query_heads = queries.reshape(SEQ, HEADS, HEAD_DIM).transpose(1, 0, 2)
    key_heads = keys.reshape(SEQ, HEADS, HEAD_DIM).transpose(1, 0, 2)
    value_heads = values.reshape(SEQ, HEADS, HEAD_DIM).transpose(1, 0, 2)
    heads_out = lax.map(lambda triple: head_attention(triple[0], triple[1], triple[2]), (query_heads, key_heads, value_heads))
    attended = heads_out[:MAIN].transpose(1, 0, 2).reshape(SEQ, MAIN * HEAD_DIM)
    leftover_heads = heads_out[MAIN:]
    counts = row_counts.astype(jnp.int32)
    exclusive = (jnp.cumsum(counts) - counts).astype(jnp.int32)
    device_ids = jnp.arange(N_ULY, dtype=jnp.int32)
    head_index = (device_ids // PER).astype(jnp.int32)
    row_start = (exclusive - exclusive[head_index * PER]).astype(jnp.int32)
    offsets = jnp.arange(MOST, dtype=jnp.int32)
    within = jnp.clip(row_start[:, None] + offsets[None, :], 0, GROUP - 1).astype(jnp.int32)
    block_ids = jnp.arange(N_BLK, dtype=jnp.int32)
    row_ids = (block_ids[:, None, None] * GROUP + within[None, :, :]).astype(jnp.int32)
    picked = leftover_heads[head_index[None, :, None], row_ids]
    valid = offsets[None, :] < counts[:, None]
    picked = jnp.where(valid[None, :, :, None], picked, jnp.zeros_like(picked))
    leftover_rows = picked.reshape(N_BLK * N_ULY * MOST, HEAD_DIM)
    return attended, leftover_rows
```

```python
import functools

import jax
import jax.numpy as jnp
from jax import lax
from jax.experimental import pallas as pl
from jax.experimental.pallas import tpu as pltpu
from jax.sharding import PartitionSpec as P

ZH, ZL, NY, NX = 2, 4, 4, 4
NZ = ZH * ZL
NP = NZ * NY
TOK = 32
D = 128
ROWS = 3 * TOK
MOST = 448
MAIN = 0
LEFT = 1
QB = 256
EXP2_SCALE = D ** (-0.5) * 1.4426950408889634


def kernel(
    counts_ref, q_ref, k_ref, v_ref, att_ref, left_ref,
    send_main, send_left, kv, acc, top, out_main, out_left, got_main, got_left,
    s1m_send, s1m_recv, s1l_send, s1l_recv, yg_send, yg_recv,
    x_send, x_recv, c_send, c_recv, lo_send, lo_recv, om_send, om_recv,
):
    u = lax.axis_index("uly")
    b = lax.axis_index("blk")
    y = lax.rem(u, NY)
    zl = u // NY
    c = lax.rem(b, 2)
    x = lax.rem(b // 2, NX)
    zh = b // (2 * NX)
    z = zh * ZL + zl
    me = z * NY + y
    right = lax.rem(x + 1, NX)
    left = lax.rem(x + NX - 1, NX)
    far = lax.rem(x + 2, NX)

    def dev(x_, c_, z_, y_):
        return {"uly": lax.rem(z_, ZL) * NY + y_, "blk": ((z_ // ZL) * NX + x_) * 2 + c_}

    def dev_p(p):
        return dev(x, c, p // NY, lax.rem(p, NY))

    def remote(src, dst, ss, rs, to):
        return pltpu.make_async_remote_copy(
            src_ref=src, dst_ref=dst, send_sem=ss, recv_sem=rs,
            device_id=to, device_id_type=pl.DeviceIdType.MESH,
        )

    barrier = pltpu.get_barrier_semaphore()

    def greet(i, _):
        pl.semaphore_signal(barrier, inc=1, device_id=dev_p(lax.rem(me + i, NP)),
                            device_id_type=pl.DeviceIdType.MESH)
        return 0

    lax.fori_loop(1, NP, greet, 0)
    for to in (dev(right, c, z, y), dev(left, c, z, y), dev(x, 1 - c, z, y)):
        pl.semaphore_signal(barrier, inc=1, device_id=to, device_id_type=pl.DeviceIdType.MESH)

    for zz in range(NZ):
        head = NP + (zz % ZL) * (NY // 2) + zz // ZL
        for n, ref in enumerate((q_ref, k_ref, v_ref)):
            send_left[zz, n * TOK:(n + 1) * TOK, :] = ref[:, head * D:(head + 1) * D]
    pl.semaphore_wait(barrier, NP - 1 + 3)

    def send_l(i, _):
        to = lax.rem(z + i, NZ)
        remote(send_left.at[to], kv.at[c, x, LEFT, y * NZ + z], s1l_send.at[to], s1l_recv.at[z],
               dev(x, c, to, y)).start()
        return 0

    lax.fori_loop(1, NZ, send_l, 0)
    for p in range(NP):
        for n, ref in enumerate((q_ref, k_ref, v_ref)):
            send_main[p, n * TOK:(n + 1) * TOK, :] = ref[:, p * D:(p + 1) * D]

    def send_m(i, _):
        to = lax.rem(me + i, NP)
        remote(send_main.at[to], kv.at[c, x, MAIN, me], s1m_send.at[to], s1m_recv.at[me],
               dev_p(to)).start()
        return 0

    lax.fori_loop(1, NP, send_m, 0)
    kv[c, x, LEFT, y * NZ + z] = send_left[z]
    kv[c, x, MAIN, me] = send_main[me]
    acc[...] = jnp.zeros_like(acc)
    top[...] = jnp.full_like(top, -1e30)

    def wait_l(i, _):
        frm = lax.rem(z + i, NZ)
        remote(send_left.at[frm], kv.at[c, x, LEFT, y * NZ + frm], s1l_send.at[frm],
               s1l_recv.at[frm], dev(x, c, frm, y)).wait_recv()
        return 0

    lax.fori_loop(1, NZ, wait_l, 0)

    def yg(src_y, to_y, sem_s):
        part = kv.at[c, x, LEFT, pl.ds(src_y * NZ, NZ), pl.ds(TOK, 2 * TOK)]
        return remote(part, part, yg_send.at[sem_s], yg_recv.at[src_y], dev(x, c, z, to_y))

    for i in range(1, NY):
        to = lax.rem(y + i, NY)
        yg(y, to, to).start()
    for i in range(1, NY):
        frm = lax.rem(y + i, NY)
        yg(frm, frm, frm).wait_recv()

    def part_of(cc, xx, h, lo, n):
        return kv.at[cc, xx, h, pl.ds(lo, n), pl.ds(TOK, 2 * TOK)]

    half = NP // 2

    def x_copy(h, kind, xx, to):
        lo, n = ((0, NP), (0, NP), (0, half), (half, half))[kind]
        part = part_of(c, xx, h, lo, n)
        return remote(part, part, x_send.at[h, kind], x_recv.at[h, kind], dev(to, c, z, y))

    def c_copy(h, k, cc, xx):
        part = part_of(cc, xx, h, 0, NP)
        return remote(part, part, c_send.at[h, k], c_recv.at[h, k], dev(x, 1 - c, z, y))

    def start_own(h):
        x_copy(h, 0, x, right).start()
        x_copy(h, 1, x, left).start()
        c_copy(h, 0, c, x).start()

    def attend(h, cc, xx, row, count):
        def block(i, _):
            at = pl.multiple_of(i * QB, QB)
            src = i * (QB // TOK)
            if h == LEFT:
                src = src + y * NZ
            qq = kv[c, x, h, pl.ds(src, QB // TOK), 0:TOK, :].reshape(QB, D)
            kk = kv[cc, xx, h, :, TOK:2 * TOK, :].reshape(NP * TOK, D)
            vv = kv[cc, xx, h, :, 2 * TOK:3 * TOK, :].reshape(NP * TOK, D)
            at = at + row
            s = lax.dot_general(qq, kk, (((1,), (1,)), ((), ())), preferred_element_type=jnp.float32)
            before = top[pl.ds(at, QB), :]
            now = jnp.maximum(before, jnp.max(s, axis=1, keepdims=True))
            factor = jnp.exp2((before - now) * EXP2_SCALE)
            w = jnp.exp2((s - now[:, :1]) * EXP2_SCALE)
            top[pl.ds(at, QB), :] = now
            ones = jnp.concatenate([vv, jnp.ones_like(vv)], axis=1)
            o = jnp.dot(w.astype(jnp.bfloat16), ones, preferred_element_type=jnp.float32)
            acc[pl.ds(at, QB), :D] = acc[pl.ds(at, QB), :D] * factor + o[:, :D]
            acc[pl.ds(at, QB), D:] = acc[pl.ds(at, QB), D:] * factor + o[:, D:]
            return 0

        lax.fori_loop(0, count, block, 0, unroll=min(count, 4))

    def one_head(h, row, count, middle):
        def step(t, _):
            @pl.when(t == 1)
            def _():
                c_copy(h, 0, 1 - c, x).wait_recv()

            @pl.when(t == 2)
            def _():
                x_copy(h, 0, left, right).wait_recv()
                x_copy(h, 2, left, right).start()
                c_copy(h, 1, c, left).start()
                x_copy(h, 1, right, left).wait_recv()
                x_copy(h, 3, right, left).start()
                c_copy(h, 2, c, right).start()
                middle()

            @pl.when(t == 4)
            def _():
                c_copy(h, 1, 1 - c, left).wait_recv()
                c_copy(h, 2, 1 - c, right).wait_recv()

            @pl.when(t == 6)
            def _():
                x_copy(h, 2, far, right).wait_recv()
                x_copy(h, 3, far, left).wait_recv()
                c_copy(h, 3, c, far).start()

            @pl.when(t == 7)
            def _():
                c_copy(h, 3, 1 - c, far).wait_recv()

            flip = jnp.where((t == 1) | (t == 4) | (t == 5) | (t == 7), 1, 0)
            xx = jnp.where(t < 2, x, jnp.where(t > 5, far, jnp.where(lax.rem(t, 2) == 0, left, right)))
            attend(h, jnp.where(flip == 1, 1 - c, c), xx, row, count)
            return 0

        lax.fori_loop(0, 8, step, 0)

    def wait_m(i, _):
        frm = lax.rem(me + i, NP)
        remote(send_main.at[frm], kv.at[c, x, MAIN, frm], s1m_send.at[frm], s1m_recv.at[frm],
               dev_p(frm)).wait_recv()
        return 0

    def main_ready():
        lax.fori_loop(1, NP, wait_m, 0)
        start_own(MAIN)

    n_main = NP * TOK
    n_left = NZ * TOK
    start_own(LEFT)
    one_head(LEFT, n_main, n_left // QB, main_ready)

    res = acc[n_main:, :D] / acc[n_main:, D:]
    out_left[...] = res.astype(jnp.bfloat16).reshape(NZ, TOK, D)

    def lo_copy(zz, k):
        return remote(out_left.at[pl.ds(zz * ZL, ZL)], got_left.at[y], lo_send.at[2 * zz + k],
                      lo_recv.at[y], dev(x, c, zz * ZL + zl, 2 * zh + k))

    for zz in range(ZH):
        for k in range(2):
            own = (zz == zh) & (2 * zh + k == y)

            @pl.when(own)
            def _():
                got_left[y] = out_left[zz * ZL:(zz + 1) * ZL]

            @pl.when(jnp.logical_not(own))
            def _():
                lo_copy(zz, k).start()

    one_head(MAIN, 0, n_main // QB, lambda: None)
    res = acc[:n_main, :D] / acc[:n_main, D:]
    out_main[...] = res.astype(jnp.bfloat16).reshape(NP, TOK, D)

    def send_o(i, _):
        to = lax.rem(me + i, NP)
        remote(out_main.at[to], got_main.at[me], om_send.at[to], om_recv.at[me], dev_p(to)).start()
        return 0

    lax.fori_loop(1, NP, send_o, 0)
    got_main[me] = out_main[me]

    pair = y // 2
    for yy in range(NY):
        @pl.when(jnp.logical_not((pair == zh) & (yy == y)))
        def _():
            remote(out_left.at[pl.ds(0, ZL)], got_left.at[yy], lo_send.at[0], lo_recv.at[yy],
                   dev(x, c, pair * ZL + zl, yy)).wait_recv()
    group = ZL * NY * TOK
    mine = counts_ref[u]
    first = jnp.where(lax.rem(u, 2) == 1, counts_ref[u - lax.rem(u, 2)], 0)
    col = lax.broadcasted_iota(jnp.int32, (MOST, group), 1)
    row = lax.broadcasted_iota(jnp.int32, (MOST, group), 0)
    piece = col // TOK
    place = (lax.rem(piece, ZL) * NY + piece // ZL) * TOK + lax.rem(col, TOK)
    pick = (place == row + first) & (row < mine)
    pick = jnp.where(pick, 1.0, 0.0).astype(jnp.bfloat16)
    left_ref[...] = jnp.dot(pick, got_left[...].reshape(group, D),
                            preferred_element_type=jnp.float32).astype(jnp.bfloat16)

    def wait_o(i, _):
        frm = lax.rem(me + i, NP)
        remote(out_main.at[frm], got_main.at[frm], om_send.at[frm], om_recv.at[frm],
               dev_p(frm)).wait_recv()
        return 0

    lax.fori_loop(1, NP, wait_o, 0)
    for p in range(NP):
        att_ref[:, p * D:(p + 1) * D] = got_main[p]

    def sent_l(i, _):
        to = lax.rem(z + i, NZ)
        remote(send_left.at[to], kv.at[c, x, LEFT, y * NZ + z], s1l_send.at[to], s1l_recv.at[z],
               dev(x, c, to, y)).wait_send()
        return 0

    lax.fori_loop(1, NZ, sent_l, 0)

    def sent_m(i, _):
        to = lax.rem(me + i, NP)
        remote(send_main.at[to], kv.at[c, x, MAIN, me], s1m_send.at[to], s1m_recv.at[me],
               dev_p(to)).wait_send()
        remote(out_main.at[to], got_main.at[me], om_send.at[to], om_recv.at[me],
               dev_p(to)).wait_send()
        return 0

    lax.fori_loop(1, NP, sent_m, 0)
    for i in range(1, NY):
        to = lax.rem(y + i, NY)
        yg(y, to, to).wait_send()
    for h in (MAIN, LEFT):
        x_copy(h, 0, x, right).wait_send()
        x_copy(h, 1, x, left).wait_send()
        x_copy(h, 2, left, right).wait_send()
        x_copy(h, 3, right, left).wait_send()
        for k, xx in enumerate((x, left, right, far)):
            c_copy(h, k, c, xx).wait_send()
    for zz in range(ZH):
        for k in range(2):
            @pl.when(jnp.logical_not((zz == zh) & (2 * zh + k == y)))
            def _():
                lo_copy(zz, k).wait_send()


def per_device(queries, keys, values, row_counts):
    group = ZL * NY * TOK
    vmem = pl.BlockSpec(memory_space=pltpu.VMEM)
    rows = NP * TOK + NZ * TOK
    dma = pltpu.SemaphoreType.DMA
    bf, f32 = jnp.bfloat16, jnp.float32
    flops = 4 * rows * NX * 2 * NP * TOK * D
    return pl.pallas_call(
        kernel,
        out_shape=(
            jax.ShapeDtypeStruct((TOK, NP * D), bf),
            jax.ShapeDtypeStruct((MOST, D), bf),
        ),
        in_specs=[pl.BlockSpec(memory_space=pltpu.SMEM), vmem, vmem, vmem],
        out_specs=(vmem, vmem),
        scratch_shapes=[
            pltpu.VMEM((NP, ROWS, D), bf),
            pltpu.VMEM((NZ, ROWS, D), bf),
            pltpu.VMEM((2, NX, 2, NP, ROWS, D), bf),
            pltpu.VMEM((rows, 2 * D), f32),
            pltpu.VMEM((rows, D), f32),
            pltpu.VMEM((NP, TOK, D), bf),
            pltpu.VMEM((NZ, TOK, D), bf),
            pltpu.VMEM((NP, TOK, D), bf),
            pltpu.VMEM((NY, ZL, TOK, D), bf),
            dma((NP,)), dma((NP,)), dma((NZ,)), dma((NZ,)), dma((NY,)), dma((NY,)),
            dma((2, 4)), dma((2, 4)), dma((2, 4)), dma((2, 4)),
            dma((2 * ZH,)), dma((NY,)), dma((NP,)), dma((NP,)),
        ],
        compiler_params=pltpu.CompilerParams(
            collective_id=0, has_side_effects=True, vmem_limit_bytes=48 * 2 ** 20
        ),
        cost_estimate=pl.CostEstimate(flops=flops, bytes_accessed=2 ** 22, transcendentals=flops // 512),
    )(row_counts, queries, keys, values)


def solution(mesh):
    placed = (P(("blk", "uly"), None), P(("blk", "uly"), None), P(("blk", "uly"), None), P())
    return jax.shard_map(
        per_device,
        mesh=mesh,
        in_specs=placed,
        out_specs=(P(("blk", "uly"), None), P(("blk", "uly"), None)),
        check_vma=False,
    )
```

```python
import jax
import jax.numpy as jnp
from jax import lax
from jax.experimental import pallas as pl
from jax.experimental.pallas import tpu as pltpu
from jax.sharding import PartitionSpec as P

ZH, ZL, NY, NX = 2, 4, 4, 4
NZ = ZH * ZL
NP = NZ * NY
TOK = 32
D = 128
MOST = 448
QB = 256
LB = 64
EXP2_SCALE = D ** (-0.5) * 1.4426950408889634
MESH = pl.DeviceIdType.MESH


def kernel(
    counts_ref, q_ref, k_ref, v_ref, att_ref, left_ref,
    kvm, kvl, qm, ql, acc, top, out_main, out_left, got_left,
    s1_send, s1_recv, m_send, m_recv, mc_send, mc_recv,
    lx_send, lx_recv, ly_send, ly_recv, lc_send, lc_recv,
    lo_send, lo_recv, om_send, om_recv,
):
    u = lax.axis_index("uly")
    b = lax.axis_index("blk")
    y = lax.rem(u, NY)
    zl = u // NY
    c = lax.rem(b, 2)
    x = lax.rem(b // 2, NX)
    zh = b // (2 * NX)
    z = zh * ZL + zl
    me = z * NY + y
    half = NP // 2
    n_main = NP * TOK

    def dev(x_, c_, z_, y_):
        return {"uly": lax.rem(z_, ZL) * NY + y_, "blk": ((z_ // ZL) * NX + x_) * 2 + c_}

    def dev_p(p):
        return dev(x, c, p // NY, lax.rem(p, NY))

    def remote(src, dst, ss, rs, to):
        return pltpu.make_async_remote_copy(
            src_ref=src, dst_ref=dst, send_sem=ss, recv_sem=rs,
            device_id=to, device_id_type=MESH,
        )

    def ring(at, size):
        return lax.rem(at + 1, size), lax.rem(at + size - 1, size), lax.rem(at + 2, size)

    xr, xl, xf = ring(x, NX)
    yr, yl, yf = ring(y, NY)

    barrier = pltpu.get_barrier_semaphore()

    def greet(i, _):
        pl.semaphore_signal(barrier, inc=1, device_id=dev_p(lax.rem(me + i, NP)), device_id_type=MESH)
        return 0

    lax.fori_loop(1, NP, greet, 0)
    for to in (dev(xr, c, z, y), dev(xl, c, z, y), dev(x, 1 - c, z, y)):
        pl.semaphore_signal(barrier, inc=1, device_id=to, device_id_type=MESH)

    def columns(ref, head):
        return ref.at[:, pl.ds(pl.multiple_of(head * D, D), D)]

    def left_head(zz):
        return NP + lax.rem(zz, ZL) * (NY // 2) + zz // ZL

    own_a = 1 // (NZ // 2)
    own_at = NY % half
    own = [
        pltpu.make_async_copy(columns(k_ref, left_head(z)), kvl.at[y, c, x, z, pl.ds(0, TOK)], s1_recv.at[2]),
        pltpu.make_async_copy(columns(v_ref, left_head(z)), kvl.at[y, c, x, z, pl.ds(TOK, TOK)], s1_recv.at[2]),
        pltpu.make_async_copy(columns(k_ref, me), kvm.at[x, own_a, c, own_at + y, pl.ds(0, TOK)], s1_recv.at[own_a]),
        pltpu.make_async_copy(columns(v_ref, me), kvm.at[x, own_a, c, own_at + y, pl.ds(TOK, TOK)], s1_recv.at[own_a]),
        pltpu.make_async_copy(columns(q_ref, me), qm.at[me], s1_recv.at[3]),
        pltpu.make_async_copy(columns(q_ref, left_head(z)), ql.at[z], s1_recv.at[4]),
    ]
    for copy in own:
        copy.start()
    acc[...] = jnp.zeros_like(acc)
    top[...] = jnp.full_like(top, -1e30)
    pl.semaphore_wait(barrier, NP - 1 + 3)

    def send_lkv(i, _):
        to = lax.rem(z + i, NZ)
        for n, ref in enumerate((k_ref, v_ref)):
            remote(columns(ref, left_head(to)), kvl.at[y, c, x, z, pl.ds(n * TOK, TOK)],
                   s1_send.at[0], s1_recv.at[2], dev(x, c, to, y)).start()
        return 0

    def send_lq(i, _):
        to = lax.rem(z + i, NZ)
        remote(columns(q_ref, left_head(to)), ql.at[z], s1_send.at[1], s1_recv.at[4],
               dev(x, c, to, y)).start()
        return 0

    def send_mkv(chunk):
        def send(i, _):
            rel = i // NY
            to_z = lax.rem(z - rel + 1 + NZ, NZ)
            to_y = lax.rem(y + lax.rem(i, NY), NY)
            slot = lax.rem(rel, NZ // 2) * NY + y
            for n, ref in enumerate((k_ref, v_ref)):
                remote(columns(ref, to_z * NY + to_y), kvm.at[x, chunk, c, slot, pl.ds(n * TOK, TOK)],
                       s1_send.at[2 + n], s1_recv.at[chunk], dev(x, c, to_z, to_y)).start()
            return 0

        lo, hi = chunk * half, (chunk + 1) * half
        if lo <= NY < hi:
            lax.fori_loop(lo, NY, send, 0)
            lax.fori_loop(NY + 1, hi, send, 0)
        else:
            lax.fori_loop(lo, hi, send, 0)

    def send_mq(i, _):
        to = lax.rem(me + i, NP)
        remote(columns(q_ref, to), qm.at[me], s1_send.at[4], s1_recv.at[3], dev_p(to)).start()
        return 0

    lax.fori_loop(1, NZ, send_lkv, 0)
    send_mkv(0)
    lax.fori_loop(1, NZ, send_lq, 0)
    lax.fori_loop(1, NP, send_mq, 0)
    send_mkv(1)

    def landed(ref, sem):
        pltpu.make_async_copy(ref, ref, sem).wait()

    def m_copy(a, kind, xx, to):
        lo, n = ((0, half), (0, half), (0, half // 2), (half // 2, half // 2))[kind]
        part = kvm.at[xx, a, c, pl.ds(lo, n)]
        return remote(part, part, m_send.at[a, kind], m_recv.at[a, kind], dev(to, c, z, y))

    def mc_copy(a, k, cc, xx):
        part = kvm.at[xx, a, cc]
        return remote(part, part, mc_send.at[a, k], mc_recv.at[a, k], dev(x, 1 - c, z, y))

    def lx_copy(kind, xx, to):
        lo, n = ((0, NZ), (0, NZ), (0, NZ // 2), (NZ // 2, NZ // 2))[kind]
        part = kvl.at[y, c, xx, pl.ds(lo, n)]
        return remote(part, part, lx_send.at[kind], lx_recv.at[kind], dev(to, c, z, y))

    def ly_copy(kind, yy, to):
        lo, n = ((0, NX), (0, NX), (0, NX // 2), (NX // 2, NX // 2))[kind]
        part = kvl.at[yy, c, pl.ds(lo, n)]
        return remote(part, part, ly_send.at[kind], ly_recv.at[kind], dev(x, c, z, to))

    def lc_copy(k, cc, yy):
        part = kvl.at[yy, cc]
        return remote(part, part, lc_send.at[k], lc_recv.at[k], dev(x, 1 - c, z, y))

    def main_own(a):
        landed(kvm.at[x, a, c], s1_recv.at[a])
        m_copy(a, 0, x, xr).start()
        m_copy(a, 1, x, xl).start()
        mc_copy(a, 0, c, x).start()

    def main_pass(a):
        m_copy(a, 0, xl, xr).wait_recv()
        m_copy(a, 2, xl, xr).start()
        mc_copy(a, 1, c, xl).start()
        m_copy(a, 1, xr, xl).wait_recv()
        m_copy(a, 3, xr, xl).start()
        mc_copy(a, 2, c, xr).start()

    def main_far(a):
        m_copy(a, 2, xf, xr).wait_recv()
        m_copy(a, 3, xf, xl).wait_recv()
        mc_copy(a, 3, c, xf).start()

    def update(qq, kk, vv, at, n):
        s = lax.dot_general(qq, kk, (((1,), (1,)), ((), ())), preferred_element_type=jnp.float32)
        before = top[pl.ds(at, n), :]
        now = jnp.maximum(before, jnp.max(s, axis=1, keepdims=True))
        factor = jnp.exp2((before - now) * EXP2_SCALE)
        w = jnp.exp2((s - now[:, :1]) * EXP2_SCALE)
        top[pl.ds(at, n), :] = now
        ones = jnp.concatenate([vv, jnp.ones_like(vv)], axis=1)
        o = jnp.dot(w.astype(jnp.bfloat16), ones, preferred_element_type=jnp.float32)
        acc[pl.ds(at, n), :D] = acc[pl.ds(at, n), :D] * factor + o[:, :D]
        acc[pl.ds(at, n), D:] = acc[pl.ds(at, n), D:] * factor + o[:, D:]

    def attend_main(xx, a):
        def block(i, _):
            at = pl.multiple_of(i * QB, QB)
            qq = qm[pl.ds(i * (QB // TOK), QB // TOK)].reshape(QB, D)
            kk = kvm[xx, a, :, :, 0:TOK, :].reshape(NP * TOK, D)
            vv = kvm[xx, a, :, :, TOK:2 * TOK, :].reshape(NP * TOK, D)
            update(qq, kk, vv, at, QB)
            return 0

        lax.fori_loop(0, n_main // QB, block, 0, unroll=min(n_main // QB, 4))

    def attend_left(yy):
        def block(i, _):
            at = pl.multiple_of(n_main + i * LB, LB)
            qq = ql[pl.ds(i * (LB // TOK), LB // TOK)].reshape(LB, D)
            kk = kvl[yy, :, :, :, 0:TOK, :].reshape(2 * NX * NZ * TOK, D)
            vv = kvl[yy, :, :, :, TOK:2 * TOK, :].reshape(2 * NX * NZ * TOK, D)
            update(qq, kk, vv, at, LB)
            return 0

        count = NZ * TOK // LB
        lax.fori_loop(0, count, block, 0, unroll=min(count, 4))

    landed(kvl.at[y, c, x], s1_recv.at[2])
    lx_copy(0, x, xr).start()
    lx_copy(1, x, xl).start()
    main_own(0)
    lx_copy(0, xl, xr).wait_recv()
    lx_copy(2, xl, xr).start()
    lx_copy(1, xr, xl).wait_recv()
    lx_copy(3, xr, xl).start()
    lx_copy(2, xf, xr).wait_recv()
    lx_copy(3, xf, xl).wait_recv()
    ly_copy(0, y, yr).start()
    if NY > 2:
        ly_copy(1, y, yl).start()
    lc_copy(0, c, y).start()
    main_pass(0)
    landed(qm, s1_recv.at[3])
    landed(ql, s1_recv.at[4])

    def step(t, _):
        @pl.when(t == 0)
        def _():
            mc_copy(0, 0, 1 - c, x).wait_recv()

        @pl.when(t == 1)
        def _():
            ly_copy(0, yl, yr).wait_recv()
            lc_copy(1, c, yl).start()
            if NY > 2:
                ly_copy(2, yl, yr).start()
                ly_copy(1, yr, yl).wait_recv()
                ly_copy(3, yr, yl).start()
                lc_copy(2, c, yr).start()
            main_far(0)
            mc_copy(0, 1, 1 - c, xl).wait_recv()

        @pl.when(t == 2)
        def _():
            main_own(1)
            mc_copy(0, 2, 1 - c, xr).wait_recv()

        @pl.when(t == 3)
        def _():
            mc_copy(0, 3, 1 - c, xf).wait_recv()

        @pl.when(t == 4)
        def _():
            if NY > 2:
                ly_copy(2, yf, yr).wait_recv()
                ly_copy(3, yf, yl).wait_recv()
                lc_copy(3, c, yf).start()
            mc_copy(1, 0, 1 - c, x).wait_recv()

        @pl.when(t == 5)
        def _():
            main_pass(1)
            mc_copy(1, 1, 1 - c, xl).wait_recv()

        @pl.when(t == 6)
        def _():
            main_far(1)
            mc_copy(1, 2, 1 - c, xr).wait_recv()

        @pl.when(t == 7)
        def _():
            mc_copy(1, 3, 1 - c, xf).wait_recv()

        i = lax.rem(t, 4)
        xx = jnp.where(i == 0, x, jnp.where(i == 1, xl, jnp.where(i == 2, xr, xf)))
        attend_main(xx, t // 4)

        def left_step(j, _):
            @pl.when(j == 0)
            def _():
                lc_copy(0, 1 - c, y).wait_recv()

            @pl.when(j == 1)
            def _():
                lc_copy(1, 1 - c, yl).wait_recv()
                if NY > 2:
                    lc_copy(2, 1 - c, yr).wait_recv()

            if NY > 2:
                @pl.when(j == 3)
                def _():
                    lc_copy(3, 1 - c, yf).wait_recv()

            attend_left(jnp.where(j == 0, y, jnp.where(j == 1, yl, jnp.where(j == 2, yr, yf))))
            return 0

        lo = jnp.where(t == 0, 0, jnp.where(t == 2, 1, jnp.where(t == 4, 3, 0)))
        hi = jnp.where(t == 0, 1, jnp.where(t == 2, 3, jnp.where(t == 4, 4, 0)))
        lax.fori_loop(jnp.minimum(lo, NY), jnp.minimum(hi, NY), left_step, 0)

        @pl.when(t == 4)
        def _():
            send_left_out()

        return 0

    def lo_copy(zz, k):
        return remote(out_left.at[pl.ds(zz * ZL, ZL)], got_left.at[y], lo_send.at[2 * zz + k],
                      lo_recv.at[y], dev(x, c, zz * ZL + zl, 2 * zh + k))

    def send_left_out():
        res = acc[n_main:, :D] / acc[n_main:, D:]
        out_left[...] = res.astype(jnp.bfloat16).reshape(NZ, TOK, D)
        for zz in range(ZH):
            for k in range(2):
                own = (zz == zh) & (2 * zh + k == y)

                @pl.when(own)
                def _():
                    got_left[y] = out_left[zz * ZL:(zz + 1) * ZL]

                @pl.when(jnp.logical_not(own))
                def _():
                    lo_copy(zz, k).start()

    lax.fori_loop(0, 8, step, 0)

    res = acc[:n_main, :D] / acc[:n_main, D:]
    out_main[...] = res.astype(jnp.bfloat16).reshape(NP, TOK, D)
    own_out = pltpu.make_async_copy(out_main.at[me], columns(att_ref, me), om_recv)
    own_out.start()

    def send_o(i, _):
        to = lax.rem(me + i, NP)
        remote(out_main.at[to], columns(att_ref, me), om_send, om_recv, dev_p(to)).start()
        return 0

    lax.fori_loop(1, NP, send_o, 0)

    pair = y // 2
    for yy in range(NY):
        @pl.when(jnp.logical_not((pair == zh) & (yy == y)))
        def _():
            remote(out_left.at[pl.ds(0, ZL)], got_left.at[yy], lo_send.at[0], lo_recv.at[yy],
                   dev(x, c, pair * ZL + zl, yy)).wait_recv()
    group = ZL * NY * TOK
    mine = counts_ref[u]
    first = jnp.where(lax.rem(u, 2) == 1, counts_ref[u - lax.rem(u, 2)], 0)
    col = lax.broadcasted_iota(jnp.int32, (MOST, group), 1)
    row = lax.broadcasted_iota(jnp.int32, (MOST, group), 0)
    piece = col // TOK
    place = (lax.rem(piece, ZL) * NY + piece // ZL) * TOK + lax.rem(col, TOK)
    pick = (place == row + first) & (row < mine)
    pick = jnp.where(pick, 1.0, 0.0).astype(jnp.bfloat16)
    left_ref[...] = jnp.dot(pick, got_left[...].reshape(group, D),
                            preferred_element_type=jnp.float32).astype(jnp.bfloat16)

    def sent(ref, sem):
        pltpu.make_async_copy(ref, ref, sem).wait()

    for n in (0, 0, 1):
        sent(qm.at[pl.ds(0, NZ - 1)], s1_send.at[n])
    for n in (2, 3, 4):
        sent(qm.at[pl.ds(0, NP - 1)], s1_send.at[n])
    for a in range(2):
        m_copy(a, 0, x, xr).wait_send()
        m_copy(a, 1, x, xl).wait_send()
        m_copy(a, 2, xl, xr).wait_send()
        m_copy(a, 3, xr, xl).wait_send()
        for k, xx in enumerate((x, xl, xr, xf)):
            mc_copy(a, k, c, xx).wait_send()
    lx_copy(0, x, xr).wait_send()
    lx_copy(1, x, xl).wait_send()
    lx_copy(2, xl, xr).wait_send()
    lx_copy(3, xr, xl).wait_send()
    ly_copy(0, y, yr).wait_send()
    lc_copy(0, c, y).wait_send()
    lc_copy(1, c, yl).wait_send()
    if NY > 2:
        ly_copy(1, y, yl).wait_send()
        ly_copy(2, yl, yr).wait_send()
        ly_copy(3, yr, yl).wait_send()
        lc_copy(2, c, yr).wait_send()
        lc_copy(3, c, yf).wait_send()
    for zz in range(ZH):
        for k in range(2):
            @pl.when(jnp.logical_not((zz == zh) & (2 * zh + k == y)))
            def _():
                lo_copy(zz, k).wait_send()
    landed(qm, om_recv)
    sent(qm.at[pl.ds(0, NP - 1)], om_send)


def per_device(queries, keys, values, row_counts):
    vmem = pl.BlockSpec(memory_space=pltpu.VMEM)
    hbm = pl.BlockSpec(memory_space=pltpu.HBM)
    rows = NP * TOK + NZ * TOK
    dma = pltpu.SemaphoreType.DMA
    bf, f32 = jnp.bfloat16, jnp.float32
    flops = 4 * rows * NX * 2 * NP * TOK * D
    return pl.pallas_call(
        kernel,
        out_shape=(
            jax.ShapeDtypeStruct((TOK, NP * D), bf),
            jax.ShapeDtypeStruct((MOST, D), bf),
        ),
        in_specs=[pl.BlockSpec(memory_space=pltpu.SMEM), hbm, hbm, hbm],
        out_specs=(hbm, vmem),
        scratch_shapes=[
            pltpu.VMEM((NX, 2, 2, NP // 2, 2 * TOK, D), bf),
            pltpu.VMEM((NY, 2, NX, NZ, 2 * TOK, D), bf),
            pltpu.VMEM((NP, TOK, D), bf),
            pltpu.VMEM((NZ, TOK, D), bf),
            pltpu.VMEM((rows, 2 * D), f32),
            pltpu.VMEM((rows, D), f32),
            pltpu.VMEM((NP, TOK, D), bf),
            pltpu.VMEM((NZ, TOK, D), bf),
            pltpu.VMEM((NY, ZL, TOK, D), bf),
            dma((5,)), dma((5,)), dma((2, 4)), dma((2, 4)), dma((2, 4)), dma((2, 4)),
            dma((4,)), dma((4,)), dma((4,)), dma((4,)), dma((4,)), dma((4,)),
            dma((2 * ZH,)), dma((NY,)), dma, dma,
        ],
        compiler_params=pltpu.CompilerParams(
            collective_id=0, has_side_effects=True, vmem_limit_bytes=48 * 2 ** 20
        ),
        cost_estimate=pl.CostEstimate(flops=flops, bytes_accessed=2 ** 22, transcendentals=flops // 512),
    )(row_counts, queries, keys, values)


def solution(mesh):
    placed = (P(("blk", "uly"), None), P(("blk", "uly"), None), P(("blk", "uly"), None), P())
    return jax.shard_map(
        per_device,
        mesh=mesh,
        in_specs=placed,
        out_specs=(P(("blk", "uly"), None), P(("blk", "uly"), None)),
        check_vma=False,
    )
```

```python
import jax
import jax.numpy as jnp
from jax import lax
from jax.experimental import pallas as pl
from jax.experimental.pallas import tpu as pltpu
from jax.sharding import PartitionSpec as P

ZH, ZL, NY, NX = 2, 4, 4, 4
NZ = ZH * ZL
NP = NZ * NY
TOK = 32
D = 128
MOST = 448
QB = 256
VMEM_LIMIT = 64 * 2 ** 20 - 2 ** 18
EXP2_SCALE = D ** (-0.5) * 1.4426950408889634
MESH = pl.DeviceIdType.MESH


def kernel(
    counts_ref, q_ref, k_ref, v_ref, att_ref, left_ref,
    kv, qs, acc, top, out_main, part_o, part_s, got_o, got_s, out_left, got_left,
    s1_send, s1_recv, m_send, m_recv, mc_send, mc_recv, lx_send, lx_recv, lc_send, lc_recv,
    lq_send, lq_recv, lp_send, lp_recv, lo_send, lo_recv, om_send, om_recv,
):
    u = lax.axis_index("uly")
    b = lax.axis_index("blk")
    y = lax.rem(u, NY)
    zl = u // NY
    c = lax.rem(b, 2)
    x = lax.rem(b // 2, NX)
    zh = b // (2 * NX)
    z = zh * ZL + zl
    me = z * NY + y
    chunks = 4 if NZ == 8 else 2
    order = (0, 1, -1, 2, 3, -2, 4, -3) if NZ == 8 else (0, 1)
    per = NP // chunks
    pairs = chunks // 2
    rows = NP * TOK
    group = NZ * TOK
    left_slot = NX * pairs

    def dev(x_, c_, z_, y_):
        return {"uly": lax.rem(z_, ZL) * NY + y_, "blk": ((z_ // ZL) * NX + x_) * 2 + c_}

    def dev_p(p):
        return dev(x, c, p // NY, lax.rem(p, NY))

    def remote(src, dst, ss, rs, to):
        return pltpu.make_async_remote_copy(
            src_ref=src, dst_ref=dst, send_sem=ss, recv_sem=rs,
            device_id=to, device_id_type=MESH,
        )

    xr, xl, xf = lax.rem(x + 1, NX), lax.rem(x + NX - 1, NX), lax.rem(x + 2, NX)

    barrier = pltpu.get_barrier_semaphore()

    def greet(i, _):
        pl.semaphore_signal(barrier, inc=1, device_id=dev_p(lax.rem(me + i, NP)), device_id_type=MESH)
        return 0

    lax.fori_loop(1, NP, greet, 0)
    for to in (dev(xr, c, z, y), dev(xl, c, z, y), dev(x, 1 - c, z, y)):
        pl.semaphore_signal(barrier, inc=1, device_id=to, device_id_type=MESH)

    def columns(ref, head):
        return ref.at[:, pl.ds(pl.multiple_of(head * D, D), D)]

    def left_head(zz):
        return NP + lax.rem(zz, ZL) * (NY // 2) + zz // ZL

    s_left, s_mq, s_lq = 4, 5, 6

    def main_rows(xx, k, cc, lo, n):
        return kv.at[xx * pairs + k // 2, pl.ds((k % 2) * 2 * per + cc * per + lo, n)]

    def left_rows(cc, xx, lo, n):
        return kv.at[left_slot + cc, pl.ds(xx * NZ + lo, n)]

    def place_main(k, src, n):
        return kv.at[x * pairs + k // 2, (k % 2) * 2 * per + c * per + src, pl.ds(n * TOK, TOK)]

    def place_left(n):
        return kv.at[left_slot + c, x * NZ + z, pl.ds(n * TOK, TOK)]

    own = [
        pltpu.make_async_copy(columns(k_ref, left_head(z)), place_left(0), s1_recv.at[s_left]),
        pltpu.make_async_copy(columns(v_ref, left_head(z)), place_left(1), s1_recv.at[s_left]),
        pltpu.make_async_copy(columns(k_ref, me), place_main(0, y, 0), s1_recv.at[0]),
        pltpu.make_async_copy(columns(v_ref, me), place_main(0, y, 1), s1_recv.at[0]),
        pltpu.make_async_copy(columns(q_ref, me), qs.at[0, me], s1_recv.at[s_mq]),
        pltpu.make_async_copy(columns(q_ref, left_head(z)), qs.at[1, y * NZ + z], s1_recv.at[s_lq]),
    ]
    for copy in own:
        copy.start()
    acc[...] = jnp.zeros_like(acc)
    top[...] = jnp.full_like(top, -1e30)
    pl.semaphore_wait(barrier, NP - 1 + 3)

    def send_lkv(i, _):
        to = lax.rem(z + i, NZ)
        for n, ref in enumerate((k_ref, v_ref)):
            remote(columns(ref, left_head(to)), place_left(n), s1_send.at[0], s1_recv.at[s_left],
                   dev(x, c, to, y)).start()
        return 0

    def send_lq(i, _):
        to = lax.rem(z + i, NZ)
        remote(columns(q_ref, left_head(to)), qs.at[1, y * NZ + z], s1_send.at[1], s1_recv.at[s_lq],
               dev(x, c, to, y)).start()
        return 0

    def send_mkv(k):
        for rel in range(k * per // NY, (k + 1) * per // NY):
            to_z = lax.rem(z - order[rel] + NZ, NZ)
            slot = (rel % (per // NY)) * NY + y

            def send(i, _):
                to_y = lax.rem(y + i, NY)
                for n, ref in enumerate((k_ref, v_ref)):
                    remote(columns(ref, to_z * NY + to_y), place_main(k, slot, n),
                           s1_send.at[2 + n], s1_recv.at[k], dev(x, c, to_z, to_y)).start()
                return 0

            lax.fori_loop(1 if rel == 0 else 0, NY, send, 0)

    def send_mq(i, _):
        to = lax.rem(me + i, NP)
        remote(columns(q_ref, to), qs.at[0, me], s1_send.at[4], s1_recv.at[s_mq], dev_p(to)).start()
        return 0

    lax.fori_loop(1, NZ, send_lkv, 0)
    for k in range(chunks // 2):
        send_mkv(k)
    lax.fori_loop(1, NZ, send_lq, 0)
    lax.fori_loop(1, NP, send_mq, 0)
    for k in range(chunks // 2, chunks):
        send_mkv(k)

    def landed(ref, sem):
        pltpu.make_async_copy(ref, ref, sem).wait()

    def m_copy(k, kind, xx, to):
        lo, n = ((0, per), (0, per), (0, per // 2), (per // 2, per // 2))[kind]
        part = main_rows(xx, k, c, lo, n)
        return remote(part, part, m_send.at[k, kind], m_recv.at[k, kind], dev(to, c, z, y))

    def mc_copy(k, i, cc, xx):
        part = main_rows(xx, k, cc, 0, per)
        return remote(part, part, mc_send.at[k, i], mc_recv.at[k, i], dev(x, 1 - c, z, y))

    def lx_copy(kind, xx, to):
        lo, n = ((0, NZ), (0, NZ), (0, NZ // 2), (NZ // 2, NZ // 2))[kind]
        part = left_rows(c, xx, lo, n)
        return remote(part, part, lx_send.at[kind], lx_recv.at[kind], dev(to, c, z, y))

    def lc_copy(cc):
        part = kv.at[left_slot + cc]
        return remote(part, part, lc_send, lc_recv, dev(x, 1 - c, z, y))

    def lq_copy(src_y, to_y):
        part = qs.at[1, pl.ds(src_y * NZ, NZ)]
        return remote(part, part, lq_send.at[to_y], lq_recv.at[src_y], dev(x, c, z, to_y))

    def lp_copies(src_y, to_y):
        at = pl.ds(pl.multiple_of(to_y * group, group), group)
        return [
            remote(part_o.at[at], got_o.at[src_y], lp_send.at[0, to_y], lp_recv.at[0, src_y], dev(x, c, z, to_y)),
            remote(part_s.at[at], got_s.at[src_y], lp_send.at[1, to_y], lp_recv.at[1, src_y], dev(x, c, z, to_y)),
        ]

    def main_own(k):
        landed(main_rows(x, k, c, 0, per), s1_recv.at[k])
        m_copy(k, 0, x, xr).start()
        m_copy(k, 1, x, xl).start()
        mc_copy(k, 0, c, x).start()

    def main_pass(k):
        m_copy(k, 0, xl, xr).wait_recv()
        m_copy(k, 2, xl, xr).start()
        mc_copy(k, 1, c, xl).start()
        m_copy(k, 1, xr, xl).wait_recv()
        m_copy(k, 3, xr, xl).start()
        mc_copy(k, 2, c, xr).start()

    def main_far(k):
        m_copy(k, 2, xf, xr).wait_recv()
        m_copy(k, 3, xf, xl).wait_recv()
        mc_copy(k, 3, c, xf).start()

    def main_across(pair, i):
        for k in (2 * pair, 2 * pair + 1):
            mc_copy(k, i, 1 - c, (x, xl, xr, xf)[i]).wait_recv()

    def update(head, slot, i):
        at = pl.multiple_of(i * QB, QB)
        if not isinstance(head, int) or head:
            at = pl.multiple_of(head * rows + at, QB)
        n = QB // TOK
        qq = qs[head, pl.ds(i * n, n)].reshape(QB, D)
        kk = kv[slot, :, 0:TOK, :].reshape(4 * per * TOK, D)
        vv = kv[slot, :, TOK:2 * TOK, :].reshape(4 * per * TOK, D)
        s = lax.dot_general(qq, kk, (((1,), (1,)), ((), ())), preferred_element_type=jnp.float32)
        before = top[pl.ds(at, QB), :]
        now = jnp.maximum(before, jnp.max(s, axis=1, keepdims=True))
        factor = jnp.exp2((before - now) * EXP2_SCALE)
        w = jnp.exp2((s - now[:, :1]) * EXP2_SCALE)
        ones = jnp.concatenate([vv, jnp.ones_like(vv)], axis=1)
        o = jnp.dot(w.astype(jnp.bfloat16), ones, preferred_element_type=jnp.float32)
        return at, now, acc[pl.ds(at, QB), :D] * factor + o[:, :D], acc[pl.ds(at, QB), D:] * factor + o[:, D:]

    def attend(head, slot):
        def block(i, _):
            at, now, total, weight = update(head, slot, i)
            top[pl.ds(at, QB), :] = now
            acc[pl.ds(at, QB), :D] = total
            acc[pl.ds(at, QB), D:] = weight
            return 0

        lax.fori_loop(0, rows // QB, block, 0, unroll=True)

    def send_partial():
        at = pl.ds(rows, rows)
        weight = acc[at, D:]
        part_o[...] = (acc[at, :D] / weight).astype(jnp.bfloat16)
        part_s[...] = top[at, :] * EXP2_SCALE + jnp.log2(weight)
        for i in range(1, NY):
            to = lax.rem(y + i, NY)
            for copy in lp_copies(y, to):
                copy.start()
        mine = pl.ds(pl.multiple_of(y * group, group), group)
        got_o[y] = part_o[mine]
        got_s[y] = part_s[mine]

    def lo_copy(zz, k):
        return remote(out_left.at[pl.ds(zz * ZL, ZL)], got_left.at[y], lo_send.at[2 * zz + k],
                      lo_recv.at[y], dev(x, c, zz * ZL + zl, 2 * zh + k))

    def merge_left():
        for i in range(1, NY):
            frm = lax.rem(y + i, NY)
            for copy in lp_copies(frm, frm):
                copy.wait_recv()
        best = got_s[0]
        for yy in range(1, NY):
            best = jnp.maximum(best, got_s[yy])
        total = jnp.zeros((group, D), jnp.float32)
        weight = jnp.zeros((group, D), jnp.float32)
        for yy in range(NY):
            share = jnp.exp2(got_s[yy] - best)
            weight = weight + share
            total = total + share * got_o[yy].astype(jnp.float32)
        out_left[...] = (total / weight).astype(jnp.bfloat16).reshape(NZ, TOK, D)
        for zz in range(ZH):
            for k in range(2):
                here = (zz == zh) & (2 * zh + k == y)

                @pl.when(here)
                def _():
                    got_left[y] = out_left[zz * ZL:(zz + 1) * ZL]

                @pl.when(jnp.logical_not(here))
                def _():
                    lo_copy(zz, k).start()

    landed(left_rows(c, x, 0, NZ), s1_recv.at[s_left])
    lx_copy(0, x, xr).start()
    lx_copy(1, x, xl).start()
    main_own(0)
    lx_copy(0, xl, xr).wait_recv()
    lx_copy(2, xl, xr).start()
    lx_copy(1, xr, xl).wait_recv()
    lx_copy(3, xr, xl).start()
    main_own(1)
    landed(qs.at[1, pl.ds(y * NZ, NZ)], s1_recv.at[s_lq])
    for i in range(1, NY):
        to = lax.rem(y + i, NY)
        lq_copy(y, to).start()
    main_pass(0)
    lx_copy(2, xf, xr).wait_recv()
    lx_copy(3, xf, xl).wait_recv()
    lc_copy(c).start()
    main_pass(1)
    main_far(0)
    landed(qs.at[0], s1_recv.at[s_mq])

    def ready_own(pair):
        main_across(pair, 0)

    def before_left():
        main_far(1)
        for i in range(1, NY):
            frm = lax.rem(y + i, NY)
            lq_copy(frm, frm).wait_recv()

    def before_left_across():
        lc_copy(1 - c).wait_recv()

    xs = (x, xl, xr, xf)
    plan = [
        (0, x * pairs, lambda: main_across(0, 0)),
        (1, left_slot + c, before_left),
        (1, left_slot + 1 - c, before_left_across),
    ]

    def first_neighbour():
        main_across(0, 1)
        send_partial()

    def second_neighbour():
        main_across(0, 2)
        if pairs > 1:
            main_own(2)

    def first_far():
        main_across(0, 3)
        if pairs > 1:
            main_own(3)
            main_pass(2)
        else:
            merge_left()

    plan += [
        (0, xl * pairs, first_neighbour),
        (0, xr * pairs, second_neighbour),
        (0, xf * pairs, first_far),
    ]
    if pairs > 1:
        def second_own():
            merge_left()
            main_far(2)
            main_across(1, 0)

        def second_left():
            main_pass(3)
            main_across(1, 1)

        def second_right():
            main_far(3)
            main_across(1, 2)

        plan += [
            (0, x * pairs + 1, second_own),
            (0, xl * pairs + 1, second_left),
            (0, xr * pairs + 1, second_right),
            (0, xf * pairs + 1, lambda: main_across(1, 3)),
        ]

    def chosen(t, values):
        out = values[0]
        for i in range(1, len(values)):
            out = jnp.where(t == i, values[i], out)
        return out

    def step(t, _):
        for i, (head, slot, first) in enumerate(plan[:-1]):
            pl.when(t == i)(first)
        attend(chosen(t, [p[0] for p in plan[:-1]]), chosen(t, [p[1] for p in plan[:-1]]))
        return 0

    lax.fori_loop(0, len(plan) - 1, step, 0)

    def send_out(p):
        remote(out_main.at[p], columns(att_ref, me), om_send, om_recv, dev_p(p)).start()

    plan[-1][2]()
    parts = 2

    def last(j, _):
        for i in range(rows // QB // parts):
            blk = j * (rows // QB // parts) + i
            at, now, total, weight = update(0, plan[-1][1], blk)
            out_main[pl.ds(blk * (QB // TOK), QB // TOK)] = (
                (total / weight).astype(jnp.bfloat16).reshape(QB // TOK, TOK, D))

        def send(i, _):
            p = j * (NP // parts) + i

            @pl.when(p == me)
            def _():
                pltpu.make_async_copy(out_main.at[me], columns(att_ref, me), om_recv).start()

            @pl.when(p != me)
            def _():
                send_out(p)

            return 0

        lax.fori_loop(0, NP // parts, send, 0)
        return 0

    lax.fori_loop(0, parts, last, 0)

    pair_y = y // 2
    for yy in range(NY):
        @pl.when(jnp.logical_not((pair_y == zh) & (yy == y)))
        def _():
            remote(out_left.at[pl.ds(0, ZL)], got_left.at[yy], lo_send.at[0], lo_recv.at[yy],
                   dev(x, c, pair_y * ZL + zl, yy)).wait_recv()
    block_rows = ZL * NY * TOK
    mine = counts_ref[u]
    first = jnp.where(lax.rem(u, 2) == 1, counts_ref[u - lax.rem(u, 2)], 0)
    col = lax.broadcasted_iota(jnp.int32, (MOST, block_rows), 1)
    row = lax.broadcasted_iota(jnp.int32, (MOST, block_rows), 0)
    piece = col // TOK
    place = (lax.rem(piece, ZL) * NY + piece // ZL) * TOK + lax.rem(col, TOK)
    pick = (place == row + first) & (row < mine)
    pick = jnp.where(pick, 1.0, 0.0).astype(jnp.bfloat16)
    left_ref[...] = jnp.dot(pick, got_left[...].reshape(block_rows, D),
                            preferred_element_type=jnp.float32).astype(jnp.bfloat16)

    for n in (0, 0, 1):
        landed(qs.at[0, pl.ds(0, NZ - 1)], s1_send.at[n])
    for n in (2, 3, 4):
        landed(qs.at[0, pl.ds(0, NP - 1)], s1_send.at[n])
    for k in range(chunks):
        m_copy(k, 0, x, xr).wait_send()
        m_copy(k, 1, x, xl).wait_send()
        m_copy(k, 2, xl, xr).wait_send()
        m_copy(k, 3, xr, xl).wait_send()
        for i in range(4):
            mc_copy(k, i, c, xs[i]).wait_send()
    lx_copy(0, x, xr).wait_send()
    lx_copy(1, x, xl).wait_send()
    lx_copy(2, xl, xr).wait_send()
    lx_copy(3, xr, xl).wait_send()
    lc_copy(c).wait_send()
    for i in range(1, NY):
        to = lax.rem(y + i, NY)
        lq_copy(y, to).wait_send()
        for copy in lp_copies(y, to):
            copy.wait_send()
    for zz in range(ZH):
        for k in range(2):
            @pl.when(jnp.logical_not((zz == zh) & (2 * zh + k == y)))
            def _():
                lo_copy(zz, k).wait_send()
    landed(qs.at[0], om_recv)
    landed(qs.at[0, pl.ds(0, NP - 1)], om_send)


def per_device(queries, keys, values, row_counts):
    vmem = pl.BlockSpec(memory_space=pltpu.VMEM)
    hbm = pl.BlockSpec(memory_space=pltpu.HBM)
    chunks = 4 if NZ == 8 else 2
    rows = NP * TOK
    group = NZ * TOK
    dma = pltpu.SemaphoreType.DMA
    bf, f32 = jnp.bfloat16, jnp.float32
    flops = 4 * rows * (NX * chunks // 2 + 2) * rows * D
    return pl.pallas_call(
        kernel,
        out_shape=(
            jax.ShapeDtypeStruct((TOK, NP * D), bf),
            jax.ShapeDtypeStruct((MOST, D), bf),
        ),
        in_specs=[pl.BlockSpec(memory_space=pltpu.SMEM), hbm, hbm, hbm],
        out_specs=(hbm, vmem),
        scratch_shapes=[
            pltpu.VMEM((NX * chunks // 2 + 2, 4 * NP // chunks, 2 * TOK, D), bf),
            pltpu.VMEM((2, NP, TOK, D), bf),
            pltpu.VMEM((2 * rows, 2 * D), f32),
            pltpu.VMEM((2 * rows, D), f32),
            pltpu.VMEM((NP, TOK, D), bf),
            pltpu.VMEM((rows, D), bf),
            pltpu.VMEM((rows, D), f32),
            pltpu.VMEM((NY, group, D), bf),
            pltpu.VMEM((NY, group, D), f32),
            pltpu.VMEM((NZ, TOK, D), bf),
            pltpu.VMEM((NY, ZL, TOK, D), bf),
            dma((5,)), dma((7,)), dma((4, 4)), dma((4, 4)), dma((4, 4)), dma((4, 4)),
            dma((4,)), dma((4,)), dma, dma,
            dma((NY,)), dma((NY,)), dma((2, NY)), dma((2, NY)), dma((2 * ZH,)), dma((NY,)), dma, dma,
        ],
        compiler_params=pltpu.CompilerParams(
            collective_id=0, has_side_effects=True, vmem_limit_bytes=VMEM_LIMIT
        ),
        cost_estimate=pl.CostEstimate(flops=flops, bytes_accessed=2 ** 22, transcendentals=flops // 512),
    )(row_counts, queries, keys, values)


def solution(mesh):
    placed = (P(("blk", "uly"), None), P(("blk", "uly"), None), P(("blk", "uly"), None), P())
    return jax.shard_map(
        per_device,
        mesh=mesh,
        in_specs=placed,
        out_specs=(P(("blk", "uly"), None), P(("blk", "uly"), None)),
        check_vma=False,
    )
```

```python
import functools

import jax
import jax.numpy as jnp
from jax import lax
from jax.experimental import pallas as pl
from jax.experimental.pallas import tpu as pltpu
from jax.sharding import PartitionSpec as P

ZH, ZL, NY, NX = 2, 4, 4, 4
NZ = ZH * ZL
NP = NZ * NY
TOK = 32
D = 128
MOST = 448
QB = 128
VMEM_LIMIT = 64 * 2 ** 20 - 2 ** 18
EXP2_SCALE = D ** (-0.5) * 1.4426950408889634
MESH = pl.DeviceIdType.MESH


def kernel(
    counts_ref, q_ref, k_ref, v_ref, att_ref, left_ref,
    kv, qs, acc, top, out_main, part_o, part_s, got_o, got_s, out_left, got_left,
    s1_send, s1_recv, m_send, m_recv, mc_send, mc_recv, lx_send, lx_recv, lc_send, lc_recv,
    lq_send, lq_recv, lp_send, lp_recv, lo_send, lo_recv, om_send, om_recv,
):
    u = lax.axis_index("uly")
    b = lax.axis_index("blk")
    y = lax.rem(u, NY)
    zl = u // NY
    c = lax.rem(b, 2)
    x = lax.rem(b // 2, NX)
    zh = b // (2 * NX)
    z = zh * ZL + zl
    me = z * NY + y
    chunks = 4 if NZ == 8 else 2
    order = (0, 1, -1, 2, 3, -2, 4, -3) if NZ == 8 else (0, 1)
    per = NP // chunks
    pairs = chunks // 2
    rows = NP * TOK
    group = NZ * TOK
    left_slot = NX * pairs

    def dev(x_, c_, z_, y_):
        return {"uly": lax.rem(z_, ZL) * NY + y_, "blk": ((z_ // ZL) * NX + x_) * 2 + c_}

    def dev_p(p):
        return dev(x, c, p // NY, lax.rem(p, NY))

    def remote(src, dst, ss, rs, to):
        return pltpu.make_async_remote_copy(
            src_ref=src, dst_ref=dst, send_sem=ss, recv_sem=rs,
            device_id=to, device_id_type=MESH,
        )

    xr, xl, xf = lax.rem(x + 1, NX), lax.rem(x + NX - 1, NX), lax.rem(x + 2, NX)

    barrier = pltpu.get_barrier_semaphore()

    def greet(i, _):
        pl.semaphore_signal(barrier, inc=1, device_id=dev_p(lax.rem(me + i, NP)), device_id_type=MESH)
        return 0

    lax.fori_loop(1, NP, greet, 0)
    for to in (dev(xr, c, z, y), dev(xl, c, z, y), dev(x, 1 - c, z, y)):
        pl.semaphore_signal(barrier, inc=1, device_id=to, device_id_type=MESH)

    def columns(ref, head):
        return ref.at[:, pl.ds(pl.multiple_of(head * D, D), D)]

    def left_head(zz):
        return NP + lax.rem(zz, ZL) * (NY // 2) + zz // ZL

    s_left, s_mq, s_lq = 4, 5, 6

    def main_rows(xx, k, cc, lo, n):
        return kv.at[xx * pairs + k // 2, pl.ds((k % 2) * 2 * per + cc * per + lo, n)]

    def left_rows(cc, xx, lo, n):
        return kv.at[left_slot + cc, pl.ds(xx * NZ + lo, n)]

    def place_main(k, src, n):
        return kv.at[x * pairs + k // 2, (k % 2) * 2 * per + c * per + src, pl.ds(n * TOK, TOK)]

    def place_left(n):
        return kv.at[left_slot + c, x * NZ + z, pl.ds(n * TOK, TOK)]

    own = [
        pltpu.make_async_copy(columns(k_ref, left_head(z)), place_left(0), s1_recv.at[s_left]),
        pltpu.make_async_copy(columns(v_ref, left_head(z)), place_left(1), s1_recv.at[s_left]),
        pltpu.make_async_copy(columns(k_ref, me), place_main(0, y, 0), s1_recv.at[0]),
        pltpu.make_async_copy(columns(v_ref, me), place_main(0, y, 1), s1_recv.at[0]),
        pltpu.make_async_copy(columns(q_ref, me), qs.at[0, me], s1_recv.at[s_mq]),
        pltpu.make_async_copy(columns(q_ref, left_head(z)), qs.at[1, y * NZ + z], s1_recv.at[s_lq]),
    ]
    for copy in own:
        copy.start()
    acc[...] = jnp.zeros_like(acc)
    top[...] = jnp.full_like(top, -1e30)
    pl.semaphore_wait(barrier, NP - 1 + 3)

    def send_lkv(i, _):
        to = lax.rem(z + i, NZ)
        for n, ref in enumerate((k_ref, v_ref)):
            remote(columns(ref, left_head(to)), place_left(n), s1_send.at[0], s1_recv.at[s_left],
                   dev(x, c, to, y)).start()
        return 0

    def send_lq(i, _):
        to = lax.rem(z + i, NZ)
        remote(columns(q_ref, left_head(to)), qs.at[1, y * NZ + z], s1_send.at[1], s1_recv.at[s_lq],
               dev(x, c, to, y)).start()
        return 0

    def send_mkv(k):
        for rel in range(k * per // NY, (k + 1) * per // NY):
            to_z = lax.rem(z - order[rel] + NZ, NZ)
            slot = (rel % (per // NY)) * NY + y

            def send(i, _):
                to_y = lax.rem(y + i, NY)
                for n, ref in enumerate((k_ref, v_ref)):
                    remote(columns(ref, to_z * NY + to_y), place_main(k, slot, n),
                           s1_send.at[2 + n], s1_recv.at[k], dev(x, c, to_z, to_y)).start()
                return 0

            lax.fori_loop(1 if rel == 0 else 0, NY, send, 0)

    def send_mq(i, _):
        to = lax.rem(me + i, NP)
        remote(columns(q_ref, to), qs.at[0, me], s1_send.at[4], s1_recv.at[s_mq], dev_p(to)).start()
        return 0

    lax.fori_loop(1, NZ, send_lkv, 0)
    for k in range(chunks // 2):
        send_mkv(k)
    lax.fori_loop(1, NZ, send_lq, 0)
    lax.fori_loop(1, NP, send_mq, 0)
    for k in range(chunks // 2, chunks):
        send_mkv(k)

    def landed(ref, sem):
        pltpu.make_async_copy(ref, ref, sem).wait()

    def m_copy(k, kind, xx, to):
        lo, n = ((0, per), (0, per), (0, per // 2), (per // 2, per // 2))[kind]
        part = main_rows(xx, k, c, lo, n)
        return remote(part, part, m_send.at[k, kind], m_recv.at[k, kind], dev(to, c, z, y))

    def mc_copy(k, i, cc, xx):
        part = main_rows(xx, k, cc, 0, per)
        return remote(part, part, mc_send.at[k, i], mc_recv.at[k, i], dev(x, 1 - c, z, y))

    def lx_copy(kind, xx, to):
        lo, n = ((0, NZ), (0, NZ), (0, NZ // 2), (NZ // 2, NZ // 2))[kind]
        part = left_rows(c, xx, lo, n)
        return remote(part, part, lx_send.at[kind], lx_recv.at[kind], dev(to, c, z, y))

    def lc_copy(cc):
        part = kv.at[left_slot + cc]
        return remote(part, part, lc_send, lc_recv, dev(x, 1 - c, z, y))

    def lq_copy(src_y, to_y):
        part = qs.at[1, pl.ds(src_y * NZ, NZ)]
        return remote(part, part, lq_send.at[to_y], lq_recv.at[src_y], dev(x, c, z, to_y))

    def lp_copies(src_y, to_y):
        at = pl.ds(pl.multiple_of(to_y * group, group), group)
        return [
            remote(part_o.at[at], got_o.at[src_y], lp_send.at[0, to_y], lp_recv.at[0, src_y], dev(x, c, z, to_y)),
            remote(part_s.at[at], got_s.at[src_y], lp_send.at[1, to_y], lp_recv.at[1, src_y], dev(x, c, z, to_y)),
        ]

    def main_own(k):
        landed(main_rows(x, k, c, 0, per), s1_recv.at[k])
        m_copy(k, 0, x, xr).start()
        m_copy(k, 1, x, xl).start()
        mc_copy(k, 0, c, x).start()

    def main_pass(k):
        m_copy(k, 0, xl, xr).wait_recv()
        m_copy(k, 2, xl, xr).start()
        mc_copy(k, 1, c, xl).start()
        m_copy(k, 1, xr, xl).wait_recv()
        m_copy(k, 3, xr, xl).start()
        mc_copy(k, 2, c, xr).start()

    def main_far(k):
        m_copy(k, 2, xf, xr).wait_recv()
        m_copy(k, 3, xf, xl).wait_recv()
        mc_copy(k, 3, c, xf).start()

    def main_across(pair, i):
        for k in (2 * pair, 2 * pair + 1):
            mc_copy(k, i, 1 - c, (x, xl, xr, xf)[i]).wait_recv()

    def update(head, slot, i):
        at = pl.multiple_of(i * QB, QB)
        if not isinstance(head, int) or head:
            at = pl.multiple_of(head * rows + at, QB)
        n = QB // TOK
        qq = qs[head, pl.ds(i * n, n)].reshape(QB, D)
        kk = kv[slot, :, 0:TOK, :].reshape(4 * per * TOK, D)
        vv = kv[slot, :, TOK:2 * TOK, :].reshape(4 * per * TOK, D)
        s = lax.dot_general(qq, kk, (((1,), (1,)), ((), ())), preferred_element_type=jnp.float32)
        before = top[pl.ds(at, QB), :]
        now = jnp.maximum(before, jnp.max(s, axis=1, keepdims=True))
        factor = jnp.exp2((before - now) * EXP2_SCALE)
        w = jnp.exp2((s - now[:, :1]) * EXP2_SCALE)
        ones = jnp.concatenate([vv, jnp.ones_like(vv)], axis=1)
        o = jnp.dot(w.astype(jnp.bfloat16), ones, preferred_element_type=jnp.float32)
        return at, now, acc[pl.ds(at, QB), :D] * factor + o[:, :D], acc[pl.ds(at, QB), D:] * factor + o[:, D:]

    def attend(head, slot):
        def block(i, _):
            at, now, total, weight = update(head, slot, i)
            top[pl.ds(at, QB), :] = now
            acc[pl.ds(at, QB), :D] = total
            acc[pl.ds(at, QB), D:] = weight
            return 0

        lax.fori_loop(0, rows // QB, block, 0, unroll=True)

    def send_partial():
        at = pl.ds(rows, rows)
        weight = acc[at, D:]
        part_o[...] = (acc[at, :D] / weight).astype(jnp.bfloat16)
        part_s[...] = top[at, :] * EXP2_SCALE + jnp.log2(weight)
        for i in range(1, NY):
            to = lax.rem(y + i, NY)
            for copy in lp_copies(y, to):
                copy.start()
        mine = pl.ds(pl.multiple_of(y * group, group), group)
        got_o[y] = part_o[mine]
        got_s[y] = part_s[mine]

    def lo_copy(zz, k):
        return remote(out_left.at[pl.ds(zz * ZL, ZL)], got_left.at[y], lo_send.at[2 * zz + k],
                      lo_recv.at[y], dev(x, c, zz * ZL + zl, 2 * zh + k))

    def merge_left():
        for i in range(1, NY):
            frm = lax.rem(y + i, NY)
            for copy in lp_copies(frm, frm):
                copy.wait_recv()
        best = got_s[0]
        for yy in range(1, NY):
            best = jnp.maximum(best, got_s[yy])
        total = jnp.zeros((group, D), jnp.float32)
        weight = jnp.zeros((group, D), jnp.float32)
        for yy in range(NY):
            share = jnp.exp2(got_s[yy] - best)
            weight = weight + share
            total = total + share * got_o[yy].astype(jnp.float32)
        out_left[...] = (total / weight).astype(jnp.bfloat16).reshape(NZ, TOK, D)
        for zz in range(ZH):
            for k in range(2):
                here = (zz == zh) & (2 * zh + k == y)

                @pl.when(here)
                def _():
                    got_left[y] = out_left[zz * ZL:(zz + 1) * ZL]

                @pl.when(jnp.logical_not(here))
                def _():
                    lo_copy(zz, k).start()

    landed(left_rows(c, x, 0, NZ), s1_recv.at[s_left])
    lx_copy(0, x, xr).start()
    lx_copy(1, x, xl).start()
    main_own(0)
    lx_copy(0, xl, xr).wait_recv()
    lx_copy(2, xl, xr).start()
    lx_copy(1, xr, xl).wait_recv()
    lx_copy(3, xr, xl).start()
    main_own(1)
    landed(qs.at[1, pl.ds(y * NZ, NZ)], s1_recv.at[s_lq])
    for i in range(1, NY):
        to = lax.rem(y + i, NY)
        lq_copy(y, to).start()
    main_pass(0)
    lx_copy(2, xf, xr).wait_recv()
    lx_copy(3, xf, xl).wait_recv()
    lc_copy(c).start()
    main_pass(1)
    main_far(0)
    landed(qs.at[0], s1_recv.at[s_mq])

    def queries_over_y():
        for i in range(1, NY):
            frm = lax.rem(y + i, NY)
            lq_copy(frm, frm).wait_recv()

    xs = (x, xl, xr, xf)
    if pairs > 1:
        early = [lambda: main_own(2)]
        middle = [lambda: main_own(3), lambda: main_pass(2)]
        late = [lambda: main_pass(3), lambda: main_far(2), lambda: main_across(1, 0)]
    else:
        early, middle, late = [], [], []
    plan = [
        (0, x * pairs, [lambda: main_across(0, 0)]),
        (1, left_slot + c, [lambda: main_far(1), queries_over_y]),
        (1, left_slot + 1 - c, early + [lambda: lc_copy(1 - c).wait_recv()]),
        (0, xl * pairs, [lambda: main_across(0, 1), send_partial]),
        (0, xr * pairs, middle + [lambda: main_across(0, 2)]),
        (0, xf * pairs, [lambda: main_across(0, 3)] + ([merge_left] if pairs == 1 else [])),
    ]
    if pairs > 1:
        plan += [
            (0, x * pairs + 1, late),
            (0, xl * pairs + 1, [lambda: main_across(1, 1), merge_left]),
            (0, xr * pairs + 1, [lambda: main_far(3), lambda: main_across(1, 2)]),
            (0, xf * pairs + 1, [lambda: main_across(1, 3)]),
        ]

    def run_all(events):
        for event in events:
            event()

    def chosen(t, values):
        out = values[0]
        for i in range(1, len(values)):
            out = jnp.where(t == i, values[i], out)
        return out

    def step(t, _):
        for i, (head, slot, first) in enumerate(plan[:-1]):
            pl.when(t == i)(functools.partial(run_all, first))
        attend(chosen(t, [p[0] for p in plan[:-1]]), chosen(t, [p[1] for p in plan[:-1]]))
        return 0

    lax.fori_loop(0, len(plan) - 1, step, 0)

    def send_out(p):
        remote(out_main.at[p], columns(att_ref, me), om_send, om_recv, dev_p(p)).start()

    run_all(plan[-1][2])
    parts = min(4, NZ)
    each = NZ // parts
    turn = [d % NZ for d in ((4, 3, 5, 2, 6, 1, 7, 0) if NZ == 8 else (1, 0))]

    def last(j, _):
        planes = [lax.rem(z + chosen(j, turn[i::each]), NZ) for i in range(each)]
        for plane in planes:
            at, now, total, weight = update(0, plan[-1][1], plane)
            out_main[pl.ds(plane * NY, NY)] = (total / weight).astype(jnp.bfloat16).reshape(NY, TOK, D)
        for plane in planes:
            for i in range(NY):
                p = plane * NY + lax.rem(y + i, NY)
                if i > 0:
                    send_out(p)
                else:
                    @pl.when(p == me)
                    def _():
                        pltpu.make_async_copy(out_main.at[me], columns(att_ref, me), om_recv).start()

                    @pl.when(p != me)
                    def _():
                        send_out(p)
        return 0

    lax.fori_loop(0, parts, last, 0)

    pair_y = y // 2
    for yy in range(NY):
        @pl.when(jnp.logical_not((pair_y == zh) & (yy == y)))
        def _():
            remote(out_left.at[pl.ds(0, ZL)], got_left.at[yy], lo_send.at[0], lo_recv.at[yy],
                   dev(x, c, pair_y * ZL + zl, yy)).wait_recv()
    block_rows = ZL * NY * TOK
    mine = counts_ref[u]
    first = jnp.where(lax.rem(u, 2) == 1, counts_ref[u - lax.rem(u, 2)], 0)
    col = lax.broadcasted_iota(jnp.int32, (MOST, block_rows), 1)
    row = lax.broadcasted_iota(jnp.int32, (MOST, block_rows), 0)
    piece = col // TOK
    place = (lax.rem(piece, ZL) * NY + piece // ZL) * TOK + lax.rem(col, TOK)
    pick = (place == row + first) & (row < mine)
    pick = jnp.where(pick, 1.0, 0.0).astype(jnp.bfloat16)
    left_ref[...] = jnp.dot(pick, got_left[...].reshape(block_rows, D),
                            preferred_element_type=jnp.float32).astype(jnp.bfloat16)

    for n in (0, 0, 1):
        landed(qs.at[0, pl.ds(0, NZ - 1)], s1_send.at[n])
    for n in (2, 3, 4):
        landed(qs.at[0, pl.ds(0, NP - 1)], s1_send.at[n])
    for k in range(chunks):
        m_copy(k, 0, x, xr).wait_send()
        m_copy(k, 1, x, xl).wait_send()
        m_copy(k, 2, xl, xr).wait_send()
        m_copy(k, 3, xr, xl).wait_send()
        for i in range(4):
            mc_copy(k, i, c, xs[i]).wait_send()
    lx_copy(0, x, xr).wait_send()
    lx_copy(1, x, xl).wait_send()
    lx_copy(2, xl, xr).wait_send()
    lx_copy(3, xr, xl).wait_send()
    lc_copy(c).wait_send()
    for i in range(1, NY):
        to = lax.rem(y + i, NY)
        lq_copy(y, to).wait_send()
        for copy in lp_copies(y, to):
            copy.wait_send()
    for zz in range(ZH):
        for k in range(2):
            @pl.when(jnp.logical_not((zz == zh) & (2 * zh + k == y)))
            def _():
                lo_copy(zz, k).wait_send()
    landed(qs.at[0], om_recv)
    landed(qs.at[0, pl.ds(0, NP - 1)], om_send)


def per_device(queries, keys, values, row_counts):
    vmem = pl.BlockSpec(memory_space=pltpu.VMEM)
    hbm = pl.BlockSpec(memory_space=pltpu.HBM)
    chunks = 4 if NZ == 8 else 2
    rows = NP * TOK
    group = NZ * TOK
    dma = pltpu.SemaphoreType.DMA
    bf, f32 = jnp.bfloat16, jnp.float32
    flops = 4 * rows * (NX * chunks // 2 + 2) * rows * D
    return pl.pallas_call(
        kernel,
        out_shape=(
            jax.ShapeDtypeStruct((TOK, NP * D), bf),
            jax.ShapeDtypeStruct((MOST, D), bf),
        ),
        in_specs=[pl.BlockSpec(memory_space=pltpu.SMEM), hbm, hbm, hbm],
        out_specs=(hbm, vmem),
        scratch_shapes=[
            pltpu.VMEM((NX * chunks // 2 + 2, 4 * NP // chunks, 2 * TOK, D), bf),
            pltpu.VMEM((2, NP, TOK, D), bf),
            pltpu.VMEM((2 * rows, 2 * D), f32),
            pltpu.VMEM((2 * rows, D), f32),
            pltpu.VMEM((NP, TOK, D), bf),
            pltpu.VMEM((rows, D), bf),
            pltpu.VMEM((rows, D), f32),
            pltpu.VMEM((NY, group, D), bf),
            pltpu.VMEM((NY, group, D), f32),
            pltpu.VMEM((NZ, TOK, D), bf),
            pltpu.VMEM((NY, ZL, TOK, D), bf),
            dma((5,)), dma((7,)), dma((4, 4)), dma((4, 4)), dma((4, 4)), dma((4, 4)),
            dma((4,)), dma((4,)), dma, dma,
            dma((NY,)), dma((NY,)), dma((2, NY)), dma((2, NY)), dma((2 * ZH,)), dma((NY,)), dma, dma,
        ],
        compiler_params=pltpu.CompilerParams(
            collective_id=0, has_side_effects=True, vmem_limit_bytes=VMEM_LIMIT
        ),
        cost_estimate=pl.CostEstimate(flops=flops, bytes_accessed=2 ** 22, transcendentals=flops // 512),
    )(row_counts, queries, keys, values)


def solution(mesh):
    placed = (P(("blk", "uly"), None), P(("blk", "uly"), None), P(("blk", "uly"), None), P())
    return jax.shard_map(
        per_device,
        mesh=mesh,
        in_specs=placed,
        out_specs=(P(("blk", "uly"), None), P(("blk", "uly"), None)),
        check_vma=False,
    )
```

```python
import functools

import jax
import jax.numpy as jnp
from jax import lax
from jax.experimental import pallas as pl
from jax.experimental.pallas import tpu as pltpu
from jax.sharding import PartitionSpec as P

ZH, ZL, NY, NX = 2, 4, 4, 4
NZ = ZH * ZL
NP = NZ * NY
TOK = 32
D = 128
MOST = 448
QB = 128
VMEM_LIMIT = 64 * 2 ** 20 - 2 ** 18
EXP2_SCALE = D ** (-0.5) * 1.4426950408889634
MESH = pl.DeviceIdType.MESH


DIRECT = (2, 3, 4)


def layout():
    if NZ == 8:
        order = (0, 1, -1, 2, 3, -2, 4, -3)
        sizes = ((2, 2), (2, 1, 1))
    else:
        order, sizes = (0, 1), ((1, 1),)
    chunks = []
    for slot, each in enumerate(sizes):
        first = 0
        for n in each:
            chunks.append((slot, first, n * NY))
            first += 2 * n * NY
    return order, chunks, len(sizes)


def kernel(
    counts_ref, q_ref, k_ref, v_ref, att_ref, left_ref,
    kv, qs, acc, top, out_main, part_o, part_s, got_o, got_s, out_left, got_left,
    s1_send, s1_recv, m_send, m_recv, mc_send, mc_recv, lx_send, lx_recv, lc_send, lc_recv,
    lq_send, lq_recv, lp_send, lp_recv, lo_send, lo_recv, om_send, om_recv, ready,
):
    u = lax.axis_index("uly")
    b = lax.axis_index("blk")
    y = lax.rem(u, NY)
    zl = u // NY
    c = lax.rem(b, 2)
    x = lax.rem(b // 2, NX)
    zh = b // (2 * NX)
    z = zh * ZL + zl
    me = z * NY + y
    order, parts_of, pairs = layout()
    chunks = len(parts_of)
    direct = DIRECT
    rows = NP * TOK
    group = NZ * TOK
    left_slot = NX * pairs
    keys = kv.shape[1] * TOK

    def dev(x_, c_, z_, y_):
        return {"uly": lax.rem(z_, ZL) * NY + y_, "blk": ((z_ // ZL) * NX + x_) * 2 + c_}

    def dev_p(p):
        return dev(x, c, p // NY, lax.rem(p, NY))

    def remote(src, dst, ss, rs, to):
        return pltpu.make_async_remote_copy(
            src_ref=src, dst_ref=dst, send_sem=ss, recv_sem=rs,
            device_id=to, device_id_type=MESH,
        )

    xr, xl, xf = lax.rem(x + 1, NX), lax.rem(x + NX - 1, NX), lax.rem(x + 2, NX)

    barrier = pltpu.get_barrier_semaphore()

    def greet(i, _):
        pl.semaphore_signal(barrier, inc=1, device_id=dev(x, c, lax.rem(z + i, NZ), y), device_id_type=MESH)
        return 0

    lax.fori_loop(1, NZ, greet, 0)
    row = [dev(x, c, z, lax.rem(y + i, NY)) for i in range(1, NY)]
    near = [dev(xr, c, z, y), dev(xl, c, z, y), dev(xf, c, z, y), dev(x, 1 - c, z, y)]
    for to in row + near:
        pl.semaphore_signal(barrier, inc=1, device_id=to, device_id_type=MESH)

    def columns(ref, head):
        return ref.at[:, pl.ds(pl.multiple_of(head * D, D), D)]

    def left_head(zz):
        return NP + lax.rem(zz, ZL) * (NY // 2) + zz // ZL

    s_left, s_mq, s_lq = chunks, chunks + 1, chunks + 2

    def main_rows(xx, k, cc, lo, n):
        slot, first, size = parts_of[k]
        return kv.at[xx * pairs + slot, pl.ds(first + cc * size + lo, n)]

    def left_rows(cc, xx, lo, n):
        return kv.at[left_slot + cc, pl.ds(xx * NZ + lo, n)]

    def place_main(k, src, n):
        slot, first, size = parts_of[k]
        return kv.at[x * pairs + slot, first + c * size + src, pl.ds(n * TOK, TOK)]

    def place_left(n):
        return kv.at[left_slot + c, x * NZ + z, pl.ds(n * TOK, TOK)]

    own = [
        pltpu.make_async_copy(columns(k_ref, left_head(z)), place_left(0), s1_recv.at[s_left]),
        pltpu.make_async_copy(columns(v_ref, left_head(z)), place_left(1), s1_recv.at[s_left]),
        pltpu.make_async_copy(columns(k_ref, me), place_main(0, y, 0), s1_recv.at[0]),
        pltpu.make_async_copy(columns(v_ref, me), place_main(0, y, 1), s1_recv.at[0]),
        pltpu.make_async_copy(columns(q_ref, me), qs.at[0, me], s1_recv.at[s_mq]),
        pltpu.make_async_copy(columns(q_ref, left_head(z)), qs.at[1, y * NZ + z], s1_recv.at[s_lq]),
    ]
    for copy in own:
        copy.start()
    acc[...] = jnp.zeros_like(acc)
    top[...] = jnp.full_like(top, -1e30)
    pl.semaphore_wait(barrier, NZ - 1 + len(row) + len(near))
    for to in row:
        pl.semaphore_signal(ready, inc=1, device_id=to, device_id_type=MESH)

    def send_lkv(i, _):
        to = lax.rem(z + i, NZ)
        for n, ref in enumerate((k_ref, v_ref)):
            remote(columns(ref, left_head(to)), place_left(n), s1_send.at[0], s1_recv.at[s_left],
                   dev(x, c, to, y)).start()
        return 0

    def send_lq(i, _):
        to = lax.rem(z + i, NZ)
        remote(columns(q_ref, left_head(to)), qs.at[1, y * NZ + z], s1_send.at[1], s1_recv.at[s_lq],
               dev(x, c, to, y)).start()
        return 0

    def send_mkv(k):
        before = sum(part[2] for part in parts_of[:k]) // NY
        for rel in range(before, before + parts_of[k][2] // NY):
            to_z = lax.rem(z - order[rel] + NZ, NZ)
            slot = (rel - before) * NY + y

            def send(i, _):
                to_y = lax.rem(y + i, NY)
                for n, ref in enumerate((k_ref, v_ref)):
                    remote(columns(ref, to_z * NY + to_y), place_main(k, slot, n),
                           s1_send.at[2 + n], s1_recv.at[k], dev(x, c, to_z, to_y)).start()
                return 0

            lax.fori_loop(1 if rel == 0 else 0, NY, send, 0)

    def send_mq(i, _):
        to = lax.rem(me + i, NP)
        remote(columns(q_ref, to), qs.at[0, me], s1_send.at[4], s1_recv.at[s_mq], dev_p(to)).start()
        return 0

    lax.fori_loop(1, NZ, send_lkv, 0)
    pl.semaphore_wait(ready, len(row))
    for k in range(2):
        send_mkv(k)
    lax.fori_loop(1, NZ, send_lq, 0)
    lax.fori_loop(1, NP, send_mq, 0)
    for k in range(2, chunks):
        send_mkv(k)

    def landed(ref, sem):
        pltpu.make_async_copy(ref, ref, sem).wait()

    def m_copy(k, kind, xx, to):
        size = parts_of[k][2]
        lo, n = ((0, size), (0, size), (0, size // 2), (size // 2, size // 2), (0, size))[kind]
        part = main_rows(xx, k, c, lo, n)
        return remote(part, part, m_send.at[k, kind], m_recv.at[k, kind], dev(to, c, z, y))

    def mc_copy(k, i, cc, xx):
        part = main_rows(xx, k, cc, 0, parts_of[k][2])
        return remote(part, part, mc_send.at[k, i], mc_recv.at[k, i], dev(x, 1 - c, z, y))

    def lx_copy(kind, xx, to):
        part = left_rows(c, xx, 0, NZ)
        return remote(part, part, lx_send.at[kind], lx_recv.at[kind], dev(to, c, z, y))

    def lc_copy(cc):
        part = kv.at[left_slot + cc]
        return remote(part, part, lc_send, lc_recv, dev(x, 1 - c, z, y))

    def lq_copy(src_y, to_y):
        part = qs.at[1, pl.ds(src_y * NZ, NZ)]
        return remote(part, part, lq_send.at[to_y], lq_recv.at[src_y], dev(x, c, z, to_y))

    def lp_copies(src_y, to_y):
        at = pl.ds(pl.multiple_of(to_y * group, group), group)
        return [
            remote(part_o.at[at], got_o.at[src_y], lp_send.at[0, to_y], lp_recv.at[0, src_y], dev(x, c, z, to_y)),
            remote(part_s.at[at], got_s.at[src_y], lp_send.at[1, to_y], lp_recv.at[1, src_y], dev(x, c, z, to_y)),
        ]

    def main_own(k):
        landed(main_rows(x, k, c, 0, parts_of[k][2]), s1_recv.at[k])
        m_copy(k, 0, x, xr).start()
        m_copy(k, 1, x, xl).start()
        if k in direct:
            m_copy(k, 4, x, xf).start()
        mc_copy(k, 0, c, x).start()

    def main_pass(k):
        m_copy(k, 0, xl, xr).wait_recv()
        if k not in direct:
            m_copy(k, 2, xl, xr).start()
        mc_copy(k, 1, c, xl).start()
        m_copy(k, 1, xr, xl).wait_recv()
        if k not in direct:
            m_copy(k, 3, xr, xl).start()
        mc_copy(k, 2, c, xr).start()

    def main_far(k):
        if k in direct:
            m_copy(k, 4, xf, xf).wait_recv()
        else:
            m_copy(k, 2, xf, xr).wait_recv()
            m_copy(k, 3, xf, xl).wait_recv()
        mc_copy(k, 3, c, xf).start()

    def main_across(pair, i):
        for k, part in enumerate(parts_of):
            if part[0] == pair:
                mc_copy(k, i, 1 - c, (x, xl, xr, xf)[i]).wait_recv()

    def update(head, slot, i):
        at = pl.multiple_of(i * QB, QB)
        if not isinstance(head, int) or head:
            at = pl.multiple_of(head * rows + at, QB)
        n = QB // TOK
        qq = qs[head, pl.ds(i * n, n)].reshape(QB, D)
        kk = kv[slot, :, 0:TOK, :].reshape(keys, D)
        vv = kv[slot, :, TOK:2 * TOK, :].reshape(keys, D)
        s = lax.dot_general(qq, kk, (((1,), (1,)), ((), ())), preferred_element_type=jnp.float32)
        before = top[pl.ds(at, QB), :]
        now = jnp.maximum(before, jnp.max(s, axis=1, keepdims=True))
        factor = jnp.exp2((before - now) * EXP2_SCALE)
        w = jnp.exp2((s - now[:, :1]) * EXP2_SCALE)
        ones = jnp.concatenate([vv, jnp.ones_like(vv)], axis=1)
        o = jnp.dot(w.astype(jnp.bfloat16), ones, preferred_element_type=jnp.float32)
        return at, now, acc[pl.ds(at, QB), :D] * factor + o[:, :D], acc[pl.ds(at, QB), D:] * factor + o[:, D:]

    def attend(head, slot):
        def block(i, _):
            at, now, total, weight = update(head, slot, i)
            top[pl.ds(at, QB), :] = now
            acc[pl.ds(at, QB), :D] = total
            acc[pl.ds(at, QB), D:] = weight
            return 0

        lax.fori_loop(0, rows // QB, block, 0, unroll=True)

    def send_partial():
        at = pl.ds(rows, rows)
        weight = acc[at, D:]
        part_o[...] = (acc[at, :D] / weight).astype(jnp.bfloat16)
        part_s[...] = top[at, :] * EXP2_SCALE + jnp.log2(weight)
        for i in range(1, NY):
            to = lax.rem(y + i, NY)
            for copy in lp_copies(y, to):
                copy.start()
        mine = pl.ds(pl.multiple_of(y * group, group), group)
        got_o[y] = part_o[mine]
        got_s[y] = part_s[mine]

    def lo_copy(zz, k):
        return remote(out_left.at[pl.ds(zz * ZL, ZL)], got_left.at[y], lo_send.at[2 * zz + k],
                      lo_recv.at[y], dev(x, c, zz * ZL + zl, 2 * zh + k))

    def merge_left():
        for i in range(1, NY):
            frm = lax.rem(y + i, NY)
            for copy in lp_copies(frm, frm):
                copy.wait_recv()
        best = got_s[0]
        for yy in range(1, NY):
            best = jnp.maximum(best, got_s[yy])
        total = jnp.zeros((group, D), jnp.float32)
        weight = jnp.zeros((group, D), jnp.float32)
        for yy in range(NY):
            share = jnp.exp2(got_s[yy] - best)
            weight = weight + share
            total = total + share * got_o[yy].astype(jnp.float32)
        out_left[...] = (total / weight).astype(jnp.bfloat16).reshape(NZ, TOK, D)
        for zz in range(ZH):
            for k in range(2):
                here = (zz == zh) & (2 * zh + k == y)

                @pl.when(here)
                def _():
                    got_left[y] = out_left[zz * ZL:(zz + 1) * ZL]

                @pl.when(jnp.logical_not(here))
                def _():
                    lo_copy(zz, k).start()

    landed(left_rows(c, x, 0, NZ), s1_recv.at[s_left])
    lx_copy(0, x, xr).start()
    lx_copy(1, x, xl).start()
    lx_copy(2, x, xf).start()
    main_own(0)
    main_own(1)
    landed(qs.at[1, pl.ds(y * NZ, NZ)], s1_recv.at[s_lq])
    for i in range(1, NY):
        to = lax.rem(y + i, NY)
        lq_copy(y, to).start()
    main_pass(0)
    lx_copy(0, xl, xr).wait_recv()
    lx_copy(1, xr, xl).wait_recv()
    lx_copy(2, xf, xf).wait_recv()
    lc_copy(c).start()
    main_pass(1)
    main_far(0)
    landed(qs.at[0], s1_recv.at[s_mq])

    def queries_over_y():
        for i in range(1, NY):
            frm = lax.rem(y + i, NY)
            lq_copy(frm, frm).wait_recv()

    xs = (x, xl, xr, xf)
    if pairs > 1:
        soon, early = [lambda: main_own(2)], [lambda: main_own(3)]
        middle = [lambda: main_own(4)]
        late = [lambda: main_pass(2), lambda: main_far(2), lambda: main_pass(3), lambda: main_across(1, 0)]
    else:
        soon, early, middle, late = [], [], [], []
    plan = [
        (0, x * pairs, [lambda: main_across(0, 0)]),
        (1, left_slot + c, [lambda: main_far(1), queries_over_y] + soon),
        (1, left_slot + 1 - c, [lambda: lc_copy(1 - c).wait_recv()]),
        (0, xl * pairs, [lambda: main_across(0, 1), send_partial] + early),
        (0, xr * pairs, middle + [lambda: main_across(0, 2)]),
        (0, xf * pairs, [lambda: main_across(0, 3)] + ([merge_left] if pairs == 1 else [])),
    ]
    if pairs > 1:
        plan += [
            (0, x * pairs + 1, late),
            (0, xl * pairs + 1, [lambda: main_pass(4), merge_left, lambda: main_across(1, 1)]),
            (0, xr * pairs + 1, [lambda: main_far(3), lambda: main_far(4), lambda: main_across(1, 2)]),
            (0, xf * pairs + 1, [lambda: main_across(1, 3)]),
        ]

    def run_all(events):
        for event in events:
            event()

    def chosen(t, values):
        out = values[0]
        for i in range(1, len(values)):
            out = jnp.where(t == i, values[i], out)
        return out

    def step(t, _):
        for i, (head, slot, first) in enumerate(plan[:-1]):
            pl.when(t == i)(functools.partial(run_all, first))
        attend(chosen(t, [p[0] for p in plan[:-1]]), chosen(t, [p[1] for p in plan[:-1]]))
        return 0

    lax.fori_loop(0, len(plan) - 1, step, 0)

    def send_out(p):
        remote(out_main.at[p], columns(att_ref, me), om_send, om_recv, dev_p(p)).start()

    run_all(plan[-1][2])
    parts = min(4, NZ)
    each = NZ // parts
    turn = [d % NZ for d in ((4, 3, 5, 2, 6, 1, 7, 0) if NZ == 8 else (1, 0))]

    def last(j, _):
        planes = [lax.rem(z + chosen(j, turn[i::each]), NZ) for i in range(each)]
        for plane in planes:
            at, now, total, weight = update(0, plan[-1][1], plane)
            out_main[pl.ds(plane * NY, NY)] = (total / weight).astype(jnp.bfloat16).reshape(NY, TOK, D)
        for plane in planes:
            for i in range(NY):
                p = plane * NY + lax.rem(y + i, NY)
                if i > 0:
                    send_out(p)
                else:
                    @pl.when(p == me)
                    def _():
                        pltpu.make_async_copy(out_main.at[me], columns(att_ref, me), om_recv).start()

                    @pl.when(p != me)
                    def _():
                        send_out(p)
        return 0

    lax.fori_loop(0, parts, last, 0)

    pair_y = y // 2
    for yy in range(NY):
        @pl.when(jnp.logical_not((pair_y == zh) & (yy == y)))
        def _():
            remote(out_left.at[pl.ds(0, ZL)], got_left.at[yy], lo_send.at[0], lo_recv.at[yy],
                   dev(x, c, pair_y * ZL + zl, yy)).wait_recv()
    block_rows = ZL * NY * TOK
    mine = counts_ref[u]
    first = jnp.where(lax.rem(u, 2) == 1, counts_ref[u - lax.rem(u, 2)], 0)
    col = lax.broadcasted_iota(jnp.int32, (MOST, block_rows), 1)
    row = lax.broadcasted_iota(jnp.int32, (MOST, block_rows), 0)
    piece = col // TOK
    place = (lax.rem(piece, ZL) * NY + piece // ZL) * TOK + lax.rem(col, TOK)
    pick = (place == row + first) & (row < mine)
    pick = jnp.where(pick, 1.0, 0.0).astype(jnp.bfloat16)
    left_ref[...] = jnp.dot(pick, got_left[...].reshape(block_rows, D),
                            preferred_element_type=jnp.float32).astype(jnp.bfloat16)

    for n in (0, 0, 1):
        landed(qs.at[0, pl.ds(0, NZ - 1)], s1_send.at[n])
    for n in (2, 3, 4):
        landed(qs.at[0, pl.ds(0, NP - 1)], s1_send.at[n])
    for k in range(chunks):
        m_copy(k, 0, x, xr).wait_send()
        m_copy(k, 1, x, xl).wait_send()
        if k in direct:
            m_copy(k, 4, x, xf).wait_send()
        else:
            m_copy(k, 2, xl, xr).wait_send()
            m_copy(k, 3, xr, xl).wait_send()
        for i in range(4):
            mc_copy(k, i, c, xs[i]).wait_send()
    lx_copy(0, x, xr).wait_send()
    lx_copy(1, x, xl).wait_send()
    lx_copy(2, x, xf).wait_send()
    lc_copy(c).wait_send()
    for i in range(1, NY):
        to = lax.rem(y + i, NY)
        lq_copy(y, to).wait_send()
        for copy in lp_copies(y, to):
            copy.wait_send()
    for zz in range(ZH):
        for k in range(2):
            @pl.when(jnp.logical_not((zz == zh) & (2 * zh + k == y)))
            def _():
                lo_copy(zz, k).wait_send()
    landed(qs.at[0], om_recv)
    landed(qs.at[0, pl.ds(0, NP - 1)], om_send)


def per_device(queries, keys, values, row_counts):
    vmem = pl.BlockSpec(memory_space=pltpu.VMEM)
    hbm = pl.BlockSpec(memory_space=pltpu.HBM)
    order, parts_of, pairs = layout()
    chunks = len(parts_of)
    slots = NX * pairs + 2
    rows = NP * TOK
    group = NZ * TOK
    dma = pltpu.SemaphoreType.DMA
    bf, f32 = jnp.bfloat16, jnp.float32
    flops = 4 * rows * slots * rows * D
    return pl.pallas_call(
        kernel,
        out_shape=(
            jax.ShapeDtypeStruct((TOK, NP * D), bf),
            jax.ShapeDtypeStruct((MOST, D), bf),
        ),
        in_specs=[pl.BlockSpec(memory_space=pltpu.SMEM), hbm, hbm, hbm],
        out_specs=(hbm, vmem),
        scratch_shapes=[
            pltpu.VMEM((slots, NX * NZ, 2 * TOK, D), bf),
            pltpu.VMEM((2, NP, TOK, D), bf),
            pltpu.VMEM((2 * rows, 2 * D), f32),
            pltpu.VMEM((2 * rows, D), f32),
            pltpu.VMEM((NP, TOK, D), bf),
            pltpu.VMEM((rows, D), bf),
            pltpu.VMEM((rows, D), f32),
            pltpu.VMEM((NY, group, D), bf),
            pltpu.VMEM((NY, group, D), f32),
            pltpu.VMEM((NZ, TOK, D), bf),
            pltpu.VMEM((NY, ZL, TOK, D), bf),
            dma((5,)), dma((chunks + 3,)), dma((chunks, 5)), dma((chunks, 5)), dma((chunks, 4)), dma((chunks, 4)),
            dma((3,)), dma((3,)), dma, dma,
            dma((NY,)), dma((NY,)), dma((2, NY)), dma((2, NY)), dma((2 * ZH,)), dma((NY,)), dma, dma, pltpu.SemaphoreType.REGULAR,
        ],
        compiler_params=pltpu.CompilerParams(
            collective_id=0, has_side_effects=True, vmem_limit_bytes=VMEM_LIMIT
        ),
        cost_estimate=pl.CostEstimate(flops=flops, bytes_accessed=2 ** 22, transcendentals=flops // 512),
    )(row_counts, queries, keys, values)


def solution(mesh):
    placed = (P(("blk", "uly"), None), P(("blk", "uly"), None), P(("blk", "uly"), None), P())
    return jax.shard_map(
        per_device,
        mesh=mesh,
        in_specs=placed,
        out_specs=(P(("blk", "uly"), None), P(("blk", "uly"), None)),
        check_vma=False,
    )
```

```python
import functools

import jax
import jax.numpy as jnp
from jax import lax
from jax.experimental import pallas as pl
from jax.experimental.pallas import tpu as pltpu
from jax.sharding import PartitionSpec as P

ZH, ZL, NY, NX = 2, 4, 4, 4
NZ = ZH * ZL
NP = NZ * NY
TOK = 32
D = 128
MOST = 448
QB = 128
VMEM_LIMIT = 64 * 2 ** 20 - 2 ** 18
EXP2_SCALE = D ** (-0.5) * 1.4426950408889634
MESH = pl.DeviceIdType.MESH


DIRECT = ()


def layout():
    if NZ == 8:
        order = (0, 1, -1, 2, 3, -2, 4, -3)
        sizes = ((2, 2), (2, 1, 1))
    else:
        order, sizes = (0, 1), ((1, 1),)
    chunks = []
    for slot, each in enumerate(sizes):
        first = 0
        for n in each:
            chunks.append((slot, first, n * NY))
            first += 2 * n * NY
    return order, chunks, len(sizes)


def kernel(
    counts_ref, q_ref, k_ref, v_ref, att_ref, left_ref,
    kv, qs, acc, top, out_main, part_o, part_s, got_o, got_s, out_left, got_left,
    s1_send, s1_recv, m_send, m_recv, mc_send, mc_recv, lx_send, lx_recv, lc_send, lc_recv,
    lq_send, lq_recv, lp_send, lp_recv, lo_send, lo_recv, om_send, om_recv, ready,
):
    u = lax.axis_index("uly")
    b = lax.axis_index("blk")
    y = lax.rem(u, NY)
    zl = u // NY
    c = lax.rem(b, 2)
    x = lax.rem(b // 2, NX)
    zh = b // (2 * NX)
    z = zh * ZL + zl
    me = z * NY + y
    order, parts_of, pairs = layout()
    chunks = len(parts_of)
    direct = DIRECT
    rows = NP * TOK
    group = NZ * TOK
    left_slot = NX * pairs
    keys = kv.shape[1] * TOK

    def dev(x_, c_, z_, y_):
        return {"uly": lax.rem(z_, ZL) * NY + y_, "blk": ((z_ // ZL) * NX + x_) * 2 + c_}

    def dev_p(p):
        return dev(x, c, p // NY, lax.rem(p, NY))

    def remote(src, dst, ss, rs, to):
        return pltpu.make_async_remote_copy(
            src_ref=src, dst_ref=dst, send_sem=ss, recv_sem=rs,
            device_id=to, device_id_type=MESH,
        )

    xr, xl, xf = lax.rem(x + 1, NX), lax.rem(x + NX - 1, NX), lax.rem(x + 2, NX)

    barrier = pltpu.get_barrier_semaphore()

    def greet(i, _):
        pl.semaphore_signal(barrier, inc=1, device_id=dev(x, c, lax.rem(z + i, NZ), y), device_id_type=MESH)
        return 0

    lax.fori_loop(1, NZ, greet, 0)
    row = [dev(x, c, z, lax.rem(y + i, NY)) for i in range(1, NY)]
    near = [dev(xr, c, z, y), dev(xl, c, z, y), dev(xf, c, z, y), dev(x, 1 - c, z, y)]
    for to in row + near:
        pl.semaphore_signal(barrier, inc=1, device_id=to, device_id_type=MESH)

    def columns(ref, head):
        return ref.at[:, pl.ds(pl.multiple_of(head * D, D), D)]

    def left_head(zz):
        return NP + lax.rem(zz, ZL) * (NY // 2) + zz // ZL

    s_left, s_mq, s_lq = chunks, chunks + 1, chunks + 2

    def main_rows(xx, k, cc, lo, n):
        slot, first, size = parts_of[k]
        return kv.at[xx * pairs + slot, pl.ds(first + cc * size + lo, n)]

    def left_rows(cc, xx, lo, n):
        return kv.at[left_slot + cc, pl.ds(xx * NZ + lo, n)]

    def place_main(k, src, n):
        slot, first, size = parts_of[k]
        return kv.at[x * pairs + slot, first + c * size + src, pl.ds(n * TOK, TOK)]

    def place_left(n):
        return kv.at[left_slot + c, x * NZ + z, pl.ds(n * TOK, TOK)]

    own = [
        pltpu.make_async_copy(columns(k_ref, left_head(z)), place_left(0), s1_recv.at[s_left]),
        pltpu.make_async_copy(columns(v_ref, left_head(z)), place_left(1), s1_recv.at[s_left]),
        pltpu.make_async_copy(columns(k_ref, me), place_main(0, y, 0), s1_recv.at[0]),
        pltpu.make_async_copy(columns(v_ref, me), place_main(0, y, 1), s1_recv.at[0]),
        pltpu.make_async_copy(columns(q_ref, me), qs.at[0, me], s1_recv.at[s_mq]),
        pltpu.make_async_copy(columns(q_ref, left_head(z)), qs.at[1, y * NZ + z], s1_recv.at[s_lq]),
    ]
    for copy in own:
        copy.start()
    acc[...] = jnp.zeros_like(acc)
    top[...] = jnp.full_like(top, -1e30)
    pl.semaphore_wait(barrier, NZ - 1 + len(row) + len(near))
    for to in row:
        pl.semaphore_signal(ready, inc=1, device_id=to, device_id_type=MESH)

    def send_lkv(i, _):
        to = lax.rem(z + i, NZ)
        for n, ref in enumerate((k_ref, v_ref)):
            remote(columns(ref, left_head(to)), place_left(n), s1_send.at[0], s1_recv.at[s_left],
                   dev(x, c, to, y)).start()
        return 0

    def send_lq(i, _):
        to = lax.rem(z + i, NZ)
        remote(columns(q_ref, left_head(to)), qs.at[1, y * NZ + z], s1_send.at[1], s1_recv.at[s_lq],
               dev(x, c, to, y)).start()
        return 0

    def send_mkv(k):
        before = sum(part[2] for part in parts_of[:k]) // NY
        for rel in range(before, before + parts_of[k][2] // NY):
            to_z = lax.rem(z - order[rel] + NZ, NZ)
            slot = (rel - before) * NY + y

            def send(i, _):
                to_y = lax.rem(y + i, NY)
                for n, ref in enumerate((k_ref, v_ref)):
                    remote(columns(ref, to_z * NY + to_y), place_main(k, slot, n),
                           s1_send.at[2 + n], s1_recv.at[k], dev(x, c, to_z, to_y)).start()
                return 0

            lax.fori_loop(1 if rel == 0 else 0, NY, send, 0)

    def send_mq(i, _):
        to = lax.rem(me + i, NP)
        remote(columns(q_ref, to), qs.at[0, me], s1_send.at[4], s1_recv.at[s_mq], dev_p(to)).start()
        return 0

    lax.fori_loop(1, NZ, send_lkv, 0)
    pl.semaphore_wait(ready, len(row))
    for k in range(2):
        send_mkv(k)
    lax.fori_loop(1, NZ, send_lq, 0)
    for k in range(2, min(3, chunks)):
        send_mkv(k)
    lax.fori_loop(1, NP, send_mq, 0)
    for k in range(3, chunks):
        send_mkv(k)

    def landed(ref, sem):
        pltpu.make_async_copy(ref, ref, sem).wait()

    def m_copy(k, kind, xx, to):
        size = parts_of[k][2]
        lo, n = ((0, size), (0, size), (0, size // 2), (size // 2, size // 2), (0, size))[kind]
        part = main_rows(xx, k, c, lo, n)
        return remote(part, part, m_send.at[k, kind], m_recv.at[k, kind], dev(to, c, z, y))

    def mc_copy(k, i, cc, xx):
        part = main_rows(xx, k, cc, 0, parts_of[k][2])
        return remote(part, part, mc_send.at[k, i], mc_recv.at[k, i], dev(x, 1 - c, z, y))

    def lx_copy(kind, xx, to):
        part = left_rows(c, xx, 0, NZ)
        return remote(part, part, lx_send.at[kind], lx_recv.at[kind], dev(to, c, z, y))

    def lc_copy(cc):
        part = kv.at[left_slot + cc]
        return remote(part, part, lc_send, lc_recv, dev(x, 1 - c, z, y))

    def lq_copy(src_y, to_y):
        part = qs.at[1, pl.ds(src_y * NZ, NZ)]
        return remote(part, part, lq_send.at[to_y], lq_recv.at[src_y], dev(x, c, z, to_y))

    def lp_copies(src_y, to_y):
        at = pl.ds(pl.multiple_of(to_y * group, group), group)
        return [
            remote(part_o.at[at], got_o.at[src_y], lp_send.at[0, to_y], lp_recv.at[0, src_y], dev(x, c, z, to_y)),
            remote(part_s.at[at], got_s.at[src_y], lp_send.at[1, to_y], lp_recv.at[1, src_y], dev(x, c, z, to_y)),
        ]

    def main_own(k):
        landed(main_rows(x, k, c, 0, parts_of[k][2]), s1_recv.at[k])
        m_copy(k, 0, x, xr).start()
        m_copy(k, 1, x, xl).start()
        if k in direct:
            m_copy(k, 4, x, xf).start()
        mc_copy(k, 0, c, x).start()

    def main_pass(k):
        m_copy(k, 0, xl, xr).wait_recv()
        if k not in direct:
            m_copy(k, 2, xl, xr).start()
        mc_copy(k, 1, c, xl).start()
        m_copy(k, 1, xr, xl).wait_recv()
        if k not in direct:
            m_copy(k, 3, xr, xl).start()
        mc_copy(k, 2, c, xr).start()

    def main_far(k):
        if k in direct:
            m_copy(k, 4, xf, xf).wait_recv()
        else:
            m_copy(k, 2, xf, xr).wait_recv()
            m_copy(k, 3, xf, xl).wait_recv()
        mc_copy(k, 3, c, xf).start()

    def main_across(pair, i):
        for k, part in enumerate(parts_of):
            if part[0] == pair:
                mc_copy(k, i, 1 - c, (x, xl, xr, xf)[i]).wait_recv()

    def update(head, slot, i):
        at = pl.multiple_of(i * QB, QB)
        if not isinstance(head, int) or head:
            at = pl.multiple_of(head * rows + at, QB)
        n = QB // TOK
        qq = qs[head, pl.ds(i * n, n)].reshape(QB, D)
        kk = kv[slot, :, 0:TOK, :].reshape(keys, D)
        vv = kv[slot, :, TOK:2 * TOK, :].reshape(keys, D)
        s = lax.dot_general(qq, kk, (((1,), (1,)), ((), ())), preferred_element_type=jnp.float32)
        before = top[pl.ds(at, QB), :]
        now = jnp.maximum(before, jnp.max(s, axis=1, keepdims=True))
        factor = jnp.exp2((before - now) * EXP2_SCALE)
        w = jnp.exp2((s - now[:, :1]) * EXP2_SCALE)
        ones = jnp.concatenate([vv, jnp.ones_like(vv)], axis=1)
        o = jnp.dot(w.astype(jnp.bfloat16), ones, preferred_element_type=jnp.float32)
        return at, now, acc[pl.ds(at, QB), :D] * factor + o[:, :D], acc[pl.ds(at, QB), D:] * factor + o[:, D:]

    def attend(head, slot):
        def block(i, _):
            at, now, total, weight = update(head, slot, i)
            top[pl.ds(at, QB), :] = now
            acc[pl.ds(at, QB), :D] = total
            acc[pl.ds(at, QB), D:] = weight
            return 0

        lax.fori_loop(0, rows // QB, block, 0, unroll=True)

    def send_partial():
        at = pl.ds(rows, rows)
        weight = acc[at, D:]
        part_o[...] = (acc[at, :D] / weight).astype(jnp.bfloat16)
        part_s[...] = top[at, :] * EXP2_SCALE + jnp.log2(weight)
        for i in range(1, NY):
            to = lax.rem(y + i, NY)
            for copy in lp_copies(y, to):
                copy.start()
        mine = pl.ds(pl.multiple_of(y * group, group), group)
        got_o[y] = part_o[mine]
        got_s[y] = part_s[mine]

    def lo_copy(zz, k):
        return remote(out_left.at[pl.ds(zz * ZL, ZL)], got_left.at[y], lo_send.at[2 * zz + k],
                      lo_recv.at[y], dev(x, c, zz * ZL + zl, 2 * zh + k))

    def merge_left():
        for i in range(1, NY):
            frm = lax.rem(y + i, NY)
            for copy in lp_copies(frm, frm):
                copy.wait_recv()
        best = got_s[0]
        for yy in range(1, NY):
            best = jnp.maximum(best, got_s[yy])
        total = jnp.zeros((group, D), jnp.float32)
        weight = jnp.zeros((group, D), jnp.float32)
        for yy in range(NY):
            share = jnp.exp2(got_s[yy] - best)
            weight = weight + share
            total = total + share * got_o[yy].astype(jnp.float32)
        out_left[...] = (total / weight).astype(jnp.bfloat16).reshape(NZ, TOK, D)
        for zz in range(ZH):
            for k in range(2):
                here = (zz == zh) & (2 * zh + k == y)

                @pl.when(here)
                def _():
                    got_left[y] = out_left[zz * ZL:(zz + 1) * ZL]

                @pl.when(jnp.logical_not(here))
                def _():
                    lo_copy(zz, k).start()

    landed(left_rows(c, x, 0, NZ), s1_recv.at[s_left])
    lx_copy(0, x, xr).start()
    lx_copy(1, x, xl).start()
    lx_copy(2, x, xf).start()
    main_own(0)
    main_own(1)
    landed(qs.at[1, pl.ds(y * NZ, NZ)], s1_recv.at[s_lq])
    for i in range(1, NY):
        to = lax.rem(y + i, NY)
        lq_copy(y, to).start()
    main_pass(0)
    lx_copy(0, xl, xr).wait_recv()
    lx_copy(1, xr, xl).wait_recv()
    lx_copy(2, xf, xf).wait_recv()
    lc_copy(c).start()
    main_pass(1)
    main_far(0)

    def queries_over_y():
        for i in range(1, NY):
            frm = lax.rem(y + i, NY)
            lq_copy(frm, frm).wait_recv()

    xs = (x, xl, xr, xf)
    def main_queries():
        landed(qs.at[0], s1_recv.at[s_mq])

    several = pairs > 1
    plan = [
        (1, left_slot + c, [queries_over_y]),
        (1, left_slot + 1 - c, [lambda: main_own(2)] * several + [lambda: lc_copy(1 - c).wait_recv()]),
        (0, x * pairs, [lambda: main_far(1), send_partial, main_queries, lambda: main_across(0, 0)]),
        (0, xl * pairs, [lambda: main_own(3), lambda: main_pass(2)] * several + [lambda: main_across(0, 1)]),
        (0, xr * pairs, [lambda: main_own(4), lambda: main_far(2)] * several + [lambda: main_across(0, 2)]),
        (0, xf * pairs, [lambda: main_pass(3)] * several + [merge_left] * (not several)
         + [lambda: main_across(0, 3)]),
    ]
    if several:
        plan += [
            (0, x * pairs + 1, [lambda: main_pass(4), lambda: main_far(3), lambda: main_across(1, 0)]),
            (0, xl * pairs + 1, [lambda: main_far(4), merge_left, lambda: main_across(1, 1)]),
            (0, xr * pairs + 1, [lambda: main_across(1, 2)]),
            (0, xf * pairs + 1, [lambda: main_across(1, 3)]),
        ]

    def run_all(events):
        for event in events:
            event()

    def chosen(t, values):
        out = values[0]
        for i in range(1, len(values)):
            out = jnp.where(t == i, values[i], out)
        return out

    def step(t, _):
        for i, (head, slot, first) in enumerate(plan[:-1]):
            pl.when(t == i)(functools.partial(run_all, first))
        attend(chosen(t, [p[0] for p in plan[:-1]]), chosen(t, [p[1] for p in plan[:-1]]))
        return 0

    lax.fori_loop(0, len(plan) - 1, step, 0)

    def send_out(p):
        remote(out_main.at[p], columns(att_ref, me), om_send, om_recv, dev_p(p)).start()

    run_all(plan[-1][2])
    parts = min(4, NZ)
    each = NZ // parts
    turn = [d % NZ for d in ((4, 3, 5, 2, 6, 1, 7, 0) if NZ == 8 else (1, 0))]

    def last(j, _):
        planes = [lax.rem(z + chosen(j, turn[i::each]), NZ) for i in range(each)]
        for plane in planes:
            at, now, total, weight = update(0, plan[-1][1], plane)
            out_main[pl.ds(plane * NY, NY)] = (total / weight).astype(jnp.bfloat16).reshape(NY, TOK, D)
        for plane in planes:
            for i in range(NY):
                p = plane * NY + lax.rem(y + i, NY)
                if i > 0:
                    send_out(p)
                else:
                    @pl.when(p == me)
                    def _():
                        pltpu.make_async_copy(out_main.at[me], columns(att_ref, me), om_recv).start()

                    @pl.when(p != me)
                    def _():
                        send_out(p)
        return 0

    lax.fori_loop(0, parts, last, 0)

    pair_y = y // 2
    for yy in range(NY):
        @pl.when(jnp.logical_not((pair_y == zh) & (yy == y)))
        def _():
            remote(out_left.at[pl.ds(0, ZL)], got_left.at[yy], lo_send.at[0], lo_recv.at[yy],
                   dev(x, c, pair_y * ZL + zl, yy)).wait_recv()
    block_rows = ZL * NY * TOK
    mine = counts_ref[u]
    first = jnp.where(lax.rem(u, 2) == 1, counts_ref[u - lax.rem(u, 2)], 0)
    col = lax.broadcasted_iota(jnp.int32, (MOST, block_rows), 1)
    row = lax.broadcasted_iota(jnp.int32, (MOST, block_rows), 0)
    piece = col // TOK
    place = (lax.rem(piece, ZL) * NY + piece // ZL) * TOK + lax.rem(col, TOK)
    pick = (place == row + first) & (row < mine)
    pick = jnp.where(pick, 1.0, 0.0).astype(jnp.bfloat16)
    left_ref[...] = jnp.dot(pick, got_left[...].reshape(block_rows, D),
                            preferred_element_type=jnp.float32).astype(jnp.bfloat16)

    for n in (0, 0, 1):
        landed(qs.at[0, pl.ds(0, NZ - 1)], s1_send.at[n])
    for n in (2, 3, 4):
        landed(qs.at[0, pl.ds(0, NP - 1)], s1_send.at[n])
    for k in range(chunks):
        m_copy(k, 0, x, xr).wait_send()
        m_copy(k, 1, x, xl).wait_send()
        if k in direct:
            m_copy(k, 4, x, xf).wait_send()
        else:
            m_copy(k, 2, xl, xr).wait_send()
            m_copy(k, 3, xr, xl).wait_send()
        for i in range(4):
            mc_copy(k, i, c, xs[i]).wait_send()
    lx_copy(0, x, xr).wait_send()
    lx_copy(1, x, xl).wait_send()
    lx_copy(2, x, xf).wait_send()
    lc_copy(c).wait_send()
    for i in range(1, NY):
        to = lax.rem(y + i, NY)
        lq_copy(y, to).wait_send()
        for copy in lp_copies(y, to):
            copy.wait_send()
    for zz in range(ZH):
        for k in range(2):
            @pl.when(jnp.logical_not((zz == zh) & (2 * zh + k == y)))
            def _():
                lo_copy(zz, k).wait_send()
    landed(qs.at[0], om_recv)
    landed(qs.at[0, pl.ds(0, NP - 1)], om_send)


def per_device(queries, keys, values, row_counts):
    vmem = pl.BlockSpec(memory_space=pltpu.VMEM)
    hbm = pl.BlockSpec(memory_space=pltpu.HBM)
    order, parts_of, pairs = layout()
    chunks = len(parts_of)
    slots = NX * pairs + 2
    rows = NP * TOK
    group = NZ * TOK
    dma = pltpu.SemaphoreType.DMA
    bf, f32 = jnp.bfloat16, jnp.float32
    flops = 4 * rows * slots * rows * D
    return pl.pallas_call(
        kernel,
        out_shape=(
            jax.ShapeDtypeStruct((TOK, NP * D), bf),
            jax.ShapeDtypeStruct((MOST, D), bf),
        ),
        in_specs=[pl.BlockSpec(memory_space=pltpu.SMEM), hbm, hbm, hbm],
        out_specs=(hbm, vmem),
        scratch_shapes=[
            pltpu.VMEM((slots, NX * NZ, 2 * TOK, D), bf),
            pltpu.VMEM((2, NP, TOK, D), bf),
            pltpu.VMEM((2 * rows, 2 * D), f32),
            pltpu.VMEM((2 * rows, D), f32),
            pltpu.VMEM((NP, TOK, D), bf),
            pltpu.VMEM((rows, D), bf),
            pltpu.VMEM((rows, D), f32),
            pltpu.VMEM((NY, group, D), bf),
            pltpu.VMEM((NY, group, D), f32),
            pltpu.VMEM((NZ, TOK, D), bf),
            pltpu.VMEM((NY, ZL, TOK, D), bf),
            dma((5,)), dma((chunks + 3,)), dma((chunks, 5)), dma((chunks, 5)), dma((chunks, 4)), dma((chunks, 4)),
            dma((3,)), dma((3,)), dma, dma,
            dma((NY,)), dma((NY,)), dma((2, NY)), dma((2, NY)), dma((2 * ZH,)), dma((NY,)), dma, dma, pltpu.SemaphoreType.REGULAR,
        ],
        compiler_params=pltpu.CompilerParams(
            collective_id=0, has_side_effects=True, vmem_limit_bytes=VMEM_LIMIT
        ),
        cost_estimate=pl.CostEstimate(flops=flops, bytes_accessed=2 ** 22, transcendentals=flops // 512),
    )(row_counts, queries, keys, values)


def solution(mesh):
    placed = (P(("blk", "uly"), None), P(("blk", "uly"), None), P(("blk", "uly"), None), P())
    return jax.shard_map(
        per_device,
        mesh=mesh,
        in_specs=placed,
        out_specs=(P(("blk", "uly"), None), P(("blk", "uly"), None)),
        check_vma=False,
    )
```

```python
import functools

import jax
import jax.numpy as jnp
from jax import lax
from jax.experimental import pallas as pl
from jax.experimental.pallas import tpu as pltpu
from jax.sharding import PartitionSpec as P

ZH, ZL, NY, NX = 2, 4, 4, 4
NZ = ZH * ZL
NP = NZ * NY
TOK = 32
D = 128
MOST = 448
QB = 128
VMEM_LIMIT = 64 * 2 ** 20 - 2 ** 18
EXP2_SCALE = D ** (-0.5) * 1.4426950408889634
MESH = pl.DeviceIdType.MESH


DIRECT = ()


def layout():
    if NZ == 8:
        order = (0, 1, -1, 2, 3, -2, 4, -3)
        sizes = ((2, 2), (2, 2))
    else:
        order, sizes = (0, 1), ((1, 1),)
    chunks = []
    for slot, each in enumerate(sizes):
        first = 0
        for n in each:
            chunks.append((slot, first, n * NY))
            first += 2 * n * NY
    return order, chunks, len(sizes)


def kernel(
    counts_ref, q_ref, k_ref, v_ref, att_ref, left_ref,
    kv, qs, acc, top, out_main, part_o, part_s, got_o, got_s, out_left, got_left,
    s1_send, s1_recv, m_send, m_recv, mc_send, mc_recv, lx_send, lx_recv, lc_send, lc_recv,
    lq_send, lq_recv, lp_send, lp_recv, lo_send, lo_recv, om_send, om_recv, ready,
):
    u = lax.axis_index("uly")
    b = lax.axis_index("blk")
    y = lax.rem(u, NY)
    zl = u // NY
    c = lax.rem(b, 2)
    x = lax.rem(b // 2, NX)
    zh = b // (2 * NX)
    z = zh * ZL + zl
    me = z * NY + y
    order, parts_of, pairs = layout()
    chunks = len(parts_of)
    direct = DIRECT
    rows = NP * TOK
    group = NZ * TOK
    left_slot = NX * pairs
    keys = kv.shape[1] * TOK

    def dev(x_, c_, z_, y_):
        return {"uly": lax.rem(z_, ZL) * NY + y_, "blk": ((z_ // ZL) * NX + x_) * 2 + c_}

    def dev_p(p):
        return dev(x, c, p // NY, lax.rem(p, NY))

    def remote(src, dst, ss, rs, to):
        return pltpu.make_async_remote_copy(
            src_ref=src, dst_ref=dst, send_sem=ss, recv_sem=rs,
            device_id=to, device_id_type=MESH,
        )

    xr, xl, xf = lax.rem(x + 1, NX), lax.rem(x + NX - 1, NX), lax.rem(x + 2, NX)

    barrier = pltpu.get_barrier_semaphore()

    def greet(i, _):
        pl.semaphore_signal(barrier, inc=1, device_id=dev(x, c, lax.rem(z + i, NZ), y), device_id_type=MESH)
        return 0

    lax.fori_loop(1, NZ, greet, 0)
    row = [dev(x, c, z, lax.rem(y + i, NY)) for i in range(1, NY)]
    near = [dev(xr, c, z, y), dev(xl, c, z, y), dev(xf, c, z, y), dev(x, 1 - c, z, y)]
    for to in row + near:
        pl.semaphore_signal(barrier, inc=1, device_id=to, device_id_type=MESH)

    def columns(ref, head):
        return ref.at[:, pl.ds(pl.multiple_of(head * D, D), D)]

    def left_head(zz):
        return NP + lax.rem(zz, ZL) * (NY // 2) + zz // ZL

    s_left, s_mq, s_lq = chunks, chunks + 1, chunks + 2

    def main_rows(xx, k, cc, lo, n):
        slot, first, size = parts_of[k]
        return kv.at[xx * pairs + slot, pl.ds(first + cc * size + lo, n)]

    def left_rows(cc, xx, lo, n):
        return kv.at[left_slot + cc, pl.ds(xx * NZ + lo, n)]

    def place_main(k, src, n):
        slot, first, size = parts_of[k]
        return kv.at[x * pairs + slot, first + c * size + src, pl.ds(n * TOK, TOK)]

    def place_left(n):
        return kv.at[left_slot + c, x * NZ + z, pl.ds(n * TOK, TOK)]

    own = [
        pltpu.make_async_copy(columns(k_ref, left_head(z)), place_left(0), s1_recv.at[s_left]),
        pltpu.make_async_copy(columns(v_ref, left_head(z)), place_left(1), s1_recv.at[s_left]),
        pltpu.make_async_copy(columns(k_ref, me), place_main(0, y, 0), s1_recv.at[0]),
        pltpu.make_async_copy(columns(v_ref, me), place_main(0, y, 1), s1_recv.at[0]),
        pltpu.make_async_copy(columns(q_ref, me), qs.at[0, me], s1_recv.at[s_mq]),
        pltpu.make_async_copy(columns(q_ref, left_head(z)), qs.at[1, y * NZ + z], s1_recv.at[s_lq]),
    ]
    for copy in own:
        copy.start()
    acc[...] = jnp.zeros_like(acc)
    top[...] = jnp.full_like(top, -1e30)
    pl.semaphore_wait(barrier, NZ - 1 + len(row) + len(near))
    for to in row:
        pl.semaphore_signal(ready, inc=1, device_id=to, device_id_type=MESH)

    def send_lkv(i, _):
        to = lax.rem(z + i, NZ)
        for n, ref in enumerate((k_ref, v_ref)):
            remote(columns(ref, left_head(to)), place_left(n), s1_send.at[0], s1_recv.at[s_left],
                   dev(x, c, to, y)).start()
        return 0

    def send_lq(i, _):
        to = lax.rem(z + i, NZ)
        remote(columns(q_ref, left_head(to)), qs.at[1, y * NZ + z], s1_send.at[1], s1_recv.at[s_lq],
               dev(x, c, to, y)).start()
        return 0

    def send_mkv(k):
        before = sum(part[2] for part in parts_of[:k]) // NY
        for rel in range(before, before + parts_of[k][2] // NY):
            to_z = lax.rem(z - order[rel] + NZ, NZ)
            slot = (rel - before) * NY + y

            def send(i, _):
                to_y = lax.rem(y + i, NY)
                for n, ref in enumerate((k_ref, v_ref)):
                    remote(columns(ref, to_z * NY + to_y), place_main(k, slot, n),
                           s1_send.at[2 + n], s1_recv.at[k], dev(x, c, to_z, to_y)).start()
                return 0

            lax.fori_loop(1 if rel == 0 else 0, NY, send, 0)

    turns = (1, 7, 2, 6, 3, 5, 4) if NZ == 8 else (1,)

    def send_mq(plane):
        def send(i, _):
            to = lax.rem(z + plane, NZ) * NY + lax.rem(y + i, NY)
            remote(columns(q_ref, to), qs.at[0, me], s1_send.at[4], s1_recv.at[s_mq], dev_p(to)).start()
            return 0

        lax.fori_loop(1 if plane == 0 else 0, NY, send, 0)

    for plane in turns:
        send_lkv(plane, 0)
    pl.semaphore_wait(ready, len(row))
    for k in range(2):
        send_mkv(k)
    for plane in turns:
        send_lq(plane, 0)
    for k in range(2, min(3, chunks)):
        send_mkv(k)
    for plane in turns[::-1] + (0,):
        send_mq(plane)
    for k in range(3, chunks):
        send_mkv(k)

    def landed(ref, sem):
        pltpu.make_async_copy(ref, ref, sem).wait()

    def m_copy(k, kind, xx, to):
        size = parts_of[k][2]
        lo, n = ((0, size), (0, size), (0, size // 2), (size // 2, size // 2), (0, size))[kind]
        part = main_rows(xx, k, c, lo, n)
        return remote(part, part, m_send.at[k, kind], m_recv.at[k, kind], dev(to, c, z, y))

    def mc_copy(k, i, cc, xx):
        part = main_rows(xx, k, cc, 0, parts_of[k][2])
        return remote(part, part, mc_send.at[k, i], mc_recv.at[k, i], dev(x, 1 - c, z, y))

    def lx_copy(kind, xx, to):
        part = left_rows(c, xx, 0, NZ)
        return remote(part, part, lx_send.at[kind], lx_recv.at[kind], dev(to, c, z, y))

    def lc_copy(cc):
        part = kv.at[left_slot + cc]
        return remote(part, part, lc_send, lc_recv, dev(x, 1 - c, z, y))

    def lq_copy(src_y, to_y):
        part = qs.at[1, pl.ds(src_y * NZ, NZ)]
        return remote(part, part, lq_send.at[to_y], lq_recv.at[src_y], dev(x, c, z, to_y))

    def lp_copies(src_y, to_y):
        at = pl.ds(pl.multiple_of(to_y * group, group), group)
        return [
            remote(part_o.at[at], got_o.at[src_y], lp_send.at[0, to_y], lp_recv.at[0, src_y], dev(x, c, z, to_y)),
            remote(part_s.at[at], got_s.at[src_y], lp_send.at[1, to_y], lp_recv.at[1, src_y], dev(x, c, z, to_y)),
        ]

    def main_own(k):
        landed(main_rows(x, k, c, 0, parts_of[k][2]), s1_recv.at[k])
        m_copy(k, 0, x, xr).start()
        m_copy(k, 1, x, xl).start()
        if k in direct:
            m_copy(k, 4, x, xf).start()
        mc_copy(k, 0, c, x).start()

    def main_pass(k):
        m_copy(k, 0, xl, xr).wait_recv()
        if k not in direct:
            m_copy(k, 2, xl, xr).start()
        mc_copy(k, 1, c, xl).start()
        m_copy(k, 1, xr, xl).wait_recv()
        if k not in direct:
            m_copy(k, 3, xr, xl).start()
        mc_copy(k, 2, c, xr).start()

    def main_far(k):
        if k in direct:
            m_copy(k, 4, xf, xf).wait_recv()
        else:
            m_copy(k, 2, xf, xr).wait_recv()
            m_copy(k, 3, xf, xl).wait_recv()
        mc_copy(k, 3, c, xf).start()

    def main_across(pair, i):
        for k, part in enumerate(parts_of):
            if part[0] == pair:
                mc_copy(k, i, 1 - c, (x, xl, xr, xf)[i]).wait_recv()

    def update(head, slot, i):
        at = pl.multiple_of(i * QB, QB)
        if not isinstance(head, int) or head:
            at = pl.multiple_of(head * rows + at, QB)
        n = QB // TOK
        qq = qs[head, pl.ds(i * n, n)].reshape(QB, D)
        kk = kv[slot, :, 0:TOK, :].reshape(keys, D)
        vv = kv[slot, :, TOK:2 * TOK, :].reshape(keys, D)
        s = lax.dot_general(qq, kk, (((1,), (1,)), ((), ())), preferred_element_type=jnp.float32)
        before = top[pl.ds(at, QB), :]
        now = jnp.maximum(before, jnp.max(s, axis=1, keepdims=True))
        factor = jnp.exp2((before - now) * EXP2_SCALE)
        w = jnp.exp2((s - now[:, :1]) * EXP2_SCALE)
        ones = jnp.concatenate([vv, jnp.ones_like(vv)], axis=1)
        o = jnp.dot(w.astype(jnp.bfloat16), ones, preferred_element_type=jnp.float32)
        return at, now, acc[pl.ds(at, QB), :D] * factor + o[:, :D], acc[pl.ds(at, QB), D:] * factor + o[:, D:]

    def attend(head, slot):
        def block(i, _):
            at, now, total, weight = update(head, slot, i)
            top[pl.ds(at, QB), :] = now
            acc[pl.ds(at, QB), :D] = total
            acc[pl.ds(at, QB), D:] = weight
            return 0

        lax.fori_loop(0, rows // QB, block, 0, unroll=True)

    def send_partial():
        at = pl.ds(rows, rows)
        weight = acc[at, D:]
        part_o[...] = (acc[at, :D] / weight).astype(jnp.bfloat16)
        part_s[...] = top[at, :] * EXP2_SCALE + jnp.log2(weight)
        for i in range(1, NY):
            to = lax.rem(y + i, NY)
            for copy in lp_copies(y, to):
                copy.start()
        mine = pl.ds(pl.multiple_of(y * group, group), group)
        got_o[y] = part_o[mine]
        got_s[y] = part_s[mine]

    def lo_copy(zz, k):
        return remote(out_left.at[pl.ds(zz * ZL, ZL)], got_left.at[y], lo_send.at[2 * zz + k],
                      lo_recv.at[y], dev(x, c, zz * ZL + zl, 2 * zh + k))

    def merge_left():
        for i in range(1, NY):
            frm = lax.rem(y + i, NY)
            for copy in lp_copies(frm, frm):
                copy.wait_recv()
        best = got_s[0]
        for yy in range(1, NY):
            best = jnp.maximum(best, got_s[yy])
        total = jnp.zeros((group, D), jnp.float32)
        weight = jnp.zeros((group, D), jnp.float32)
        for yy in range(NY):
            share = jnp.exp2(got_s[yy] - best)
            weight = weight + share
            total = total + share * got_o[yy].astype(jnp.float32)
        out_left[...] = (total / weight).astype(jnp.bfloat16).reshape(NZ, TOK, D)
        for zz in range(ZH):
            for k in range(2):
                here = (zz == zh) & (2 * zh + k == y)

                @pl.when(here)
                def _():
                    got_left[y] = out_left[zz * ZL:(zz + 1) * ZL]

                @pl.when(jnp.logical_not(here))
                def _():
                    lo_copy(zz, k).start()

    landed(left_rows(c, x, 0, NZ), s1_recv.at[s_left])
    lx_copy(0, x, xr).start()
    lx_copy(1, x, xl).start()
    lx_copy(2, x, xf).start()
    main_own(0)
    main_own(1)
    landed(qs.at[1, pl.ds(y * NZ, NZ)], s1_recv.at[s_lq])
    for i in range(1, NY):
        to = lax.rem(y + i, NY)
        lq_copy(y, to).start()
    main_pass(0)
    lx_copy(0, xl, xr).wait_recv()
    lx_copy(1, xr, xl).wait_recv()
    lx_copy(2, xf, xf).wait_recv()
    lc_copy(c).start()
    main_pass(1)
    main_far(0)

    def queries_over_y():
        for i in range(1, NY):
            frm = lax.rem(y + i, NY)
            lq_copy(frm, frm).wait_recv()

    xs = (x, xl, xr, xf)
    def main_queries():
        landed(qs.at[0], s1_recv.at[s_mq])

    several = pairs > 1
    plan = [
        (1, left_slot + c, [queries_over_y]),
        (1, left_slot + 1 - c, [lambda: main_own(2)] * several + [lambda: lc_copy(1 - c).wait_recv()]),
        (0, x * pairs, [lambda: main_far(1), send_partial, main_queries, lambda: main_across(0, 0)]),
        (0, xl * pairs, [lambda: main_own(3), lambda: main_pass(2)] * several + [lambda: main_across(0, 1)]),
        (0, xr * pairs, [lambda: main_far(2)] * several + [lambda: main_across(0, 2)]),
        (0, xf * pairs, [lambda: main_pass(3)] * several + [merge_left] * (not several)
         + [lambda: main_across(0, 3)]),
    ]
    if several:
        plan += [
            (0, x * pairs + 1, [lambda: main_across(1, 0)]),
            (0, xl * pairs + 1, [lambda: main_far(3), merge_left, lambda: main_across(1, 1)]),
            (0, xr * pairs + 1, [lambda: main_across(1, 2)]),
            (0, xf * pairs + 1, [lambda: main_across(1, 3)]),
        ]

    def run_all(events):
        for event in events:
            event()

    def chosen(t, values):
        out = values[0]
        for i in range(1, len(values)):
            out = jnp.where(t == i, values[i], out)
        return out

    def step(t, _):
        for i, (head, slot, first) in enumerate(plan[:-1]):
            pl.when(t == i)(functools.partial(run_all, first))
        attend(chosen(t, [p[0] for p in plan[:-1]]), chosen(t, [p[1] for p in plan[:-1]]))
        return 0

    lax.fori_loop(0, len(plan) - 1, step, 0)

    def send_out(p):
        remote(out_main.at[p], columns(att_ref, me), om_send, om_recv, dev_p(p)).start()

    run_all(plan[-1][2])
    parts = min(4, NZ)
    each = NZ // parts
    turn = [d % NZ for d in ((4, 3, 5, 2, 6, 1, 7, 0) if NZ == 8 else (1, 0))]

    def last(j, _):
        planes = [lax.rem(z + chosen(j, turn[i::each]), NZ) for i in range(each)]
        for plane in planes:
            at, now, total, weight = update(0, plan[-1][1], plane)
            out_main[pl.ds(plane * NY, NY)] = (total / weight).astype(jnp.bfloat16).reshape(NY, TOK, D)
        for plane in planes:
            for i in range(NY):
                p = plane * NY + lax.rem(y + i, NY)
                if i > 0:
                    send_out(p)
                else:
                    @pl.when(p == me)
                    def _():
                        pltpu.make_async_copy(out_main.at[me], columns(att_ref, me), om_recv).start()

                    @pl.when(p != me)
                    def _():
                        send_out(p)
        return 0

    lax.fori_loop(0, parts, last, 0)

    pair_y = y // 2
    for yy in range(NY):
        @pl.when(jnp.logical_not((pair_y == zh) & (yy == y)))
        def _():
            remote(out_left.at[pl.ds(0, ZL)], got_left.at[yy], lo_send.at[0], lo_recv.at[yy],
                   dev(x, c, pair_y * ZL + zl, yy)).wait_recv()
    block_rows = ZL * NY * TOK
    mine = counts_ref[u]
    first = jnp.where(lax.rem(u, 2) == 1, counts_ref[u - lax.rem(u, 2)], 0)
    col = lax.broadcasted_iota(jnp.int32, (MOST, block_rows), 1)
    row = lax.broadcasted_iota(jnp.int32, (MOST, block_rows), 0)
    piece = col // TOK
    place = (lax.rem(piece, ZL) * NY + piece // ZL) * TOK + lax.rem(col, TOK)
    pick = (place == row + first) & (row < mine)
    pick = jnp.where(pick, 1.0, 0.0).astype(jnp.bfloat16)
    left_ref[...] = jnp.dot(pick, got_left[...].reshape(block_rows, D),
                            preferred_element_type=jnp.float32).astype(jnp.bfloat16)

    for n in (0, 0, 1):
        landed(qs.at[0, pl.ds(0, NZ - 1)], s1_send.at[n])
    for n in (2, 3, 4):
        landed(qs.at[0, pl.ds(0, NP - 1)], s1_send.at[n])
    for k in range(chunks):
        m_copy(k, 0, x, xr).wait_send()
        m_copy(k, 1, x, xl).wait_send()
        if k in direct:
            m_copy(k, 4, x, xf).wait_send()
        else:
            m_copy(k, 2, xl, xr).wait_send()
            m_copy(k, 3, xr, xl).wait_send()
        for i in range(4):
            mc_copy(k, i, c, xs[i]).wait_send()
    lx_copy(0, x, xr).wait_send()
    lx_copy(1, x, xl).wait_send()
    lx_copy(2, x, xf).wait_send()
    lc_copy(c).wait_send()
    for i in range(1, NY):
        to = lax.rem(y + i, NY)
        lq_copy(y, to).wait_send()
        for copy in lp_copies(y, to):
            copy.wait_send()
    for zz in range(ZH):
        for k in range(2):
            @pl.when(jnp.logical_not((zz == zh) & (2 * zh + k == y)))
            def _():
                lo_copy(zz, k).wait_send()
    landed(qs.at[0], om_recv)
    landed(qs.at[0, pl.ds(0, NP - 1)], om_send)


def per_device(queries, keys, values, row_counts):
    vmem = pl.BlockSpec(memory_space=pltpu.VMEM)
    hbm = pl.BlockSpec(memory_space=pltpu.HBM)
    order, parts_of, pairs = layout()
    chunks = len(parts_of)
    slots = NX * pairs + 2
    rows = NP * TOK
    group = NZ * TOK
    dma = pltpu.SemaphoreType.DMA
    bf, f32 = jnp.bfloat16, jnp.float32
    flops = 4 * rows * slots * rows * D
    return pl.pallas_call(
        kernel,
        out_shape=(
            jax.ShapeDtypeStruct((TOK, NP * D), bf),
            jax.ShapeDtypeStruct((MOST, D), bf),
        ),
        in_specs=[pl.BlockSpec(memory_space=pltpu.SMEM), hbm, hbm, hbm],
        out_specs=(hbm, vmem),
        scratch_shapes=[
            pltpu.VMEM((slots, NX * NZ, 2 * TOK, D), bf),
            pltpu.VMEM((2, NP, TOK, D), bf),
            pltpu.VMEM((2 * rows, 2 * D), f32),
            pltpu.VMEM((2 * rows, D), f32),
            pltpu.VMEM((NP, TOK, D), bf),
            pltpu.VMEM((rows, D), bf),
            pltpu.VMEM((rows, D), f32),
            pltpu.VMEM((NY, group, D), bf),
            pltpu.VMEM((NY, group, D), f32),
            pltpu.VMEM((NZ, TOK, D), bf),
            pltpu.VMEM((NY, ZL, TOK, D), bf),
            dma((5,)), dma((chunks + 3,)), dma((chunks, 5)), dma((chunks, 5)), dma((chunks, 4)), dma((chunks, 4)),
            dma((3,)), dma((3,)), dma, dma,
            dma((NY,)), dma((NY,)), dma((2, NY)), dma((2, NY)), dma((2 * ZH,)), dma((NY,)), dma, dma, pltpu.SemaphoreType.REGULAR,
        ],
        compiler_params=pltpu.CompilerParams(
            collective_id=0, has_side_effects=True, vmem_limit_bytes=VMEM_LIMIT
        ),
        cost_estimate=pl.CostEstimate(flops=flops, bytes_accessed=2 ** 22, transcendentals=flops // 512),
    )(row_counts, queries, keys, values)


def solution(mesh):
    placed = (P(("blk", "uly"), None), P(("blk", "uly"), None), P(("blk", "uly"), None), P())
    return jax.shard_map(
        per_device,
        mesh=mesh,
        in_specs=placed,
        out_specs=(P(("blk", "uly"), None), P(("blk", "uly"), None)),
        check_vma=False,
    )
```

```python
import functools

import jax
import jax.numpy as jnp
from jax import lax
from jax.experimental import pallas as pl
from jax.experimental.pallas import tpu as pltpu
from jax.sharding import PartitionSpec as P

ZH, ZL, NY, NX = 2, 4, 4, 4
NZ = ZH * ZL
NP = NZ * NY
TOK = 32
D = 128
MOST = 448
QB = 128
VMEM_LIMIT = 64 * 2 ** 20 - 2 ** 18
EXP2_SCALE = D ** (-0.5) * 1.4426950408889634
MESH = pl.DeviceIdType.MESH


DIRECT = ()


def layout():
    if NZ == 8:
        order = (0, 1, -1, 2, 3, -2, -3, 4)
        sizes = ((2, 2), (3, 1))
    else:
        order, sizes = (0, 1), ((1, 1),)
    chunks = []
    for slot, each in enumerate(sizes):
        first = 0
        for n in each:
            chunks.append((slot, first, n * NY))
            first += 2 * n * NY
    return order, chunks, len(sizes)


def kernel(
    counts_ref, q_ref, k_ref, v_ref, att_ref, left_ref,
    kv, qs, acc, top, out_main, part_o, part_s, got_o, got_s, out_left, got_left,
    s1_send, s1_recv, m_send, m_recv, mc_send, mc_recv, lx_send, lx_recv, lc_send, lc_recv,
    lq_send, lq_recv, lp_send, lp_recv, lo_send, lo_recv, om_send, om_recv, ready,
):
    u = lax.axis_index("uly")
    b = lax.axis_index("blk")
    y = lax.rem(u, NY)
    zl = u // NY
    c = lax.rem(b, 2)
    x = lax.rem(b // 2, NX)
    zh = b // (2 * NX)
    z = zh * ZL + zl
    me = z * NY + y
    order, parts_of, pairs = layout()
    chunks = len(parts_of)
    direct = DIRECT
    rows = NP * TOK
    group = NZ * TOK
    left_slot = NX * pairs
    keys = kv.shape[1] * TOK

    def dev(x_, c_, z_, y_):
        return {"uly": lax.rem(z_, ZL) * NY + y_, "blk": ((z_ // ZL) * NX + x_) * 2 + c_}

    def dev_p(p):
        return dev(x, c, p // NY, lax.rem(p, NY))

    def remote(src, dst, ss, rs, to):
        return pltpu.make_async_remote_copy(
            src_ref=src, dst_ref=dst, send_sem=ss, recv_sem=rs,
            device_id=to, device_id_type=MESH,
        )

    xr, xl, xf = lax.rem(x + 1, NX), lax.rem(x + NX - 1, NX), lax.rem(x + 2, NX)

    barrier = pltpu.get_barrier_semaphore()

    def greet(i, _):
        pl.semaphore_signal(barrier, inc=1, device_id=dev(x, c, lax.rem(z + i, NZ), y), device_id_type=MESH)
        return 0

    lax.fori_loop(1, NZ, greet, 0)
    row = [dev(x, c, z, lax.rem(y + i, NY)) for i in range(1, NY)]
    near = [dev(xr, c, z, y), dev(xl, c, z, y), dev(xf, c, z, y), dev(x, 1 - c, z, y)]
    for to in row + near:
        pl.semaphore_signal(barrier, inc=1, device_id=to, device_id_type=MESH)

    def columns(ref, head):
        return ref.at[:, pl.ds(pl.multiple_of(head * D, D), D)]

    def left_head(zz):
        return NP + lax.rem(zz, ZL) * (NY // 2) + zz // ZL

    s_left, s_mq, s_lq = chunks, chunks + 1, chunks + 2

    def main_rows(xx, k, cc, lo, n):
        slot, first, size = parts_of[k]
        return kv.at[xx * pairs + slot, pl.ds(first + cc * size + lo, n)]

    def left_rows(cc, xx, lo, n):
        return kv.at[left_slot + cc, pl.ds(xx * NZ + lo, n)]

    def place_main(k, src, n):
        slot, first, size = parts_of[k]
        return kv.at[x * pairs + slot, first + c * size + src, pl.ds(n * TOK, TOK)]

    def place_left(n):
        return kv.at[left_slot + c, x * NZ + z, pl.ds(n * TOK, TOK)]

    own = [
        pltpu.make_async_copy(columns(k_ref, left_head(z)), place_left(0), s1_recv.at[s_left]),
        pltpu.make_async_copy(columns(v_ref, left_head(z)), place_left(1), s1_recv.at[s_left]),
        pltpu.make_async_copy(columns(k_ref, me), place_main(0, y, 0), s1_recv.at[0]),
        pltpu.make_async_copy(columns(v_ref, me), place_main(0, y, 1), s1_recv.at[0]),
        pltpu.make_async_copy(columns(q_ref, me), qs.at[0, me], s1_recv.at[s_mq]),
        pltpu.make_async_copy(columns(q_ref, left_head(z)), qs.at[1, y * NZ + z], s1_recv.at[s_lq]),
    ]
    for copy in own:
        copy.start()
    acc[...] = jnp.zeros_like(acc)
    top[...] = jnp.full_like(top, -1e30)
    pl.semaphore_wait(barrier, NZ - 1 + len(row) + len(near))
    for to in row:
        pl.semaphore_signal(ready, inc=1, device_id=to, device_id_type=MESH)

    def send_lkv(i, _):
        to = lax.rem(z + i, NZ)
        for n, ref in enumerate((k_ref, v_ref)):
            remote(columns(ref, left_head(to)), place_left(n), s1_send.at[0], s1_recv.at[s_left],
                   dev(x, c, to, y)).start()
        return 0

    def send_lq(i, _):
        to = lax.rem(z + i, NZ)
        remote(columns(q_ref, left_head(to)), qs.at[1, y * NZ + z], s1_send.at[1], s1_recv.at[s_lq],
               dev(x, c, to, y)).start()
        return 0

    def send_mkv(k):
        before = sum(part[2] for part in parts_of[:k]) // NY
        for rel in range(before, before + parts_of[k][2] // NY):
            to_z = lax.rem(z - order[rel] + NZ, NZ)
            slot = (rel - before) * NY + y

            def send(i, _):
                to_y = lax.rem(y + i, NY)
                for n, ref in enumerate((k_ref, v_ref)):
                    remote(columns(ref, to_z * NY + to_y), place_main(k, slot, n),
                           s1_send.at[2 + n], s1_recv.at[k], dev(x, c, to_z, to_y)).start()
                return 0

            lax.fori_loop(1 if rel == 0 else 0, NY, send, 0)

    turns = (1, 7, 2, 6, 3, 5, 4) if NZ == 8 else (1,)

    def send_mq(plane):
        def send(i, _):
            to = lax.rem(z + plane, NZ) * NY + lax.rem(y + i, NY)
            remote(columns(q_ref, to), qs.at[0, me], s1_send.at[4], s1_recv.at[s_mq], dev_p(to)).start()
            return 0

        lax.fori_loop(1 if plane == 0 else 0, NY, send, 0)

    for plane in turns:
        send_lkv(plane, 0)
    pl.semaphore_wait(ready, len(row))
    for k in range(2):
        send_mkv(k)
    for plane in turns:
        send_lq(plane, 0)
    for k in range(2, min(3, chunks)):
        send_mkv(k)
    for plane in turns[::-1] + (0,):
        send_mq(plane)
    for k in range(3, chunks):
        send_mkv(k)

    def landed(ref, sem):
        pltpu.make_async_copy(ref, ref, sem).wait()

    def m_copy(k, kind, xx, to):
        size = parts_of[k][2]
        lo, n = ((0, size), (0, size), (0, size // 2), (size // 2, size // 2), (0, size))[kind]
        part = main_rows(xx, k, c, lo, n)
        return remote(part, part, m_send.at[k, kind], m_recv.at[k, kind], dev(to, c, z, y))

    def mc_copy(k, i, cc, xx):
        part = main_rows(xx, k, cc, 0, parts_of[k][2])
        return remote(part, part, mc_send.at[k, i], mc_recv.at[k, i], dev(x, 1 - c, z, y))

    def lx_copy(kind, xx, to):
        part = left_rows(c, xx, 0, NZ)
        return remote(part, part, lx_send.at[kind], lx_recv.at[kind], dev(to, c, z, y))

    def lc_copy(cc):
        part = kv.at[left_slot + cc]
        return remote(part, part, lc_send, lc_recv, dev(x, 1 - c, z, y))

    def lq_copy(src_y, to_y):
        part = qs.at[1, pl.ds(src_y * NZ, NZ)]
        return remote(part, part, lq_send.at[to_y], lq_recv.at[src_y], dev(x, c, z, to_y))

    def lp_copies(src_y, to_y):
        at = pl.ds(pl.multiple_of(to_y * group, group), group)
        return [
            remote(part_o.at[at], got_o.at[src_y], lp_send.at[0, to_y], lp_recv.at[0, src_y], dev(x, c, z, to_y)),
            remote(part_s.at[at], got_s.at[src_y], lp_send.at[1, to_y], lp_recv.at[1, src_y], dev(x, c, z, to_y)),
        ]

    def main_own(k):
        landed(main_rows(x, k, c, 0, parts_of[k][2]), s1_recv.at[k])
        m_copy(k, 0, x, xr).start()
        m_copy(k, 1, x, xl).start()
        if k in direct:
            m_copy(k, 4, x, xf).start()
        mc_copy(k, 0, c, x).start()

    def main_pass(k):
        m_copy(k, 0, xl, xr).wait_recv()
        if k not in direct:
            m_copy(k, 2, xl, xr).start()
        mc_copy(k, 1, c, xl).start()
        m_copy(k, 1, xr, xl).wait_recv()
        if k not in direct:
            m_copy(k, 3, xr, xl).start()
        mc_copy(k, 2, c, xr).start()

    def main_far(k):
        if k in direct:
            m_copy(k, 4, xf, xf).wait_recv()
        else:
            m_copy(k, 2, xf, xr).wait_recv()
            m_copy(k, 3, xf, xl).wait_recv()
        mc_copy(k, 3, c, xf).start()

    def main_across(pair, i):
        for k, part in enumerate(parts_of):
            if part[0] == pair:
                mc_copy(k, i, 1 - c, (x, xl, xr, xf)[i]).wait_recv()

    def update(head, slot, i):
        at = pl.multiple_of(i * QB, QB)
        if not isinstance(head, int) or head:
            at = pl.multiple_of(head * rows + at, QB)
        n = QB // TOK
        qq = qs[head, pl.ds(i * n, n)].reshape(QB, D)
        kk = kv[slot, :, 0:TOK, :].reshape(keys, D)
        vv = kv[slot, :, TOK:2 * TOK, :].reshape(keys, D)
        s = lax.dot_general(qq, kk, (((1,), (1,)), ((), ())), preferred_element_type=jnp.float32)
        before = top[pl.ds(at, QB), :]
        now = jnp.maximum(before, jnp.max(s, axis=1, keepdims=True))
        factor = jnp.exp2((before - now) * EXP2_SCALE)
        w = jnp.exp2((s - now[:, :1]) * EXP2_SCALE)
        ones = jnp.concatenate([vv, jnp.ones_like(vv)], axis=1)
        o = jnp.dot(w.astype(jnp.bfloat16), ones, preferred_element_type=jnp.float32)
        return at, now, acc[pl.ds(at, QB), :D] * factor + o[:, :D], acc[pl.ds(at, QB), D:] * factor + o[:, D:]

    def attend(head, slot):
        def block(i, _):
            at, now, total, weight = update(head, slot, i)
            top[pl.ds(at, QB), :] = now
            acc[pl.ds(at, QB), :D] = total
            acc[pl.ds(at, QB), D:] = weight
            return 0

        lax.fori_loop(0, rows // QB, block, 0, unroll=True)

    def send_partial():
        at = pl.ds(rows, rows)
        weight = acc[at, D:]
        part_o[...] = (acc[at, :D] / weight).astype(jnp.bfloat16)
        part_s[...] = top[at, :] * EXP2_SCALE + jnp.log2(weight)
        for i in range(1, NY):
            to = lax.rem(y + i, NY)
            for copy in lp_copies(y, to):
                copy.start()
        mine = pl.ds(pl.multiple_of(y * group, group), group)
        got_o[y] = part_o[mine]
        got_s[y] = part_s[mine]

    def lo_copy(zz, k):
        return remote(out_left.at[pl.ds(zz * ZL, ZL)], got_left.at[y], lo_send.at[2 * zz + k],
                      lo_recv.at[y], dev(x, c, zz * ZL + zl, 2 * zh + k))

    def merge_left():
        for i in range(1, NY):
            frm = lax.rem(y + i, NY)
            for copy in lp_copies(frm, frm):
                copy.wait_recv()
        best = got_s[0]
        for yy in range(1, NY):
            best = jnp.maximum(best, got_s[yy])
        total = jnp.zeros((group, D), jnp.float32)
        weight = jnp.zeros((group, D), jnp.float32)
        for yy in range(NY):
            share = jnp.exp2(got_s[yy] - best)
            weight = weight + share
            total = total + share * got_o[yy].astype(jnp.float32)
        out_left[...] = (total / weight).astype(jnp.bfloat16).reshape(NZ, TOK, D)
        for zz in range(ZH):
            for k in range(2):
                here = (zz == zh) & (2 * zh + k == y)

                @pl.when(here)
                def _():
                    got_left[y] = out_left[zz * ZL:(zz + 1) * ZL]

                @pl.when(jnp.logical_not(here))
                def _():
                    lo_copy(zz, k).start()

    landed(left_rows(c, x, 0, NZ), s1_recv.at[s_left])
    lx_copy(0, x, xr).start()
    lx_copy(1, x, xl).start()
    lx_copy(2, x, xf).start()
    main_own(0)
    main_own(1)
    landed(qs.at[1, pl.ds(y * NZ, NZ)], s1_recv.at[s_lq])
    for i in range(1, NY):
        to = lax.rem(y + i, NY)
        lq_copy(y, to).start()
    main_pass(0)
    lx_copy(0, xl, xr).wait_recv()
    lx_copy(1, xr, xl).wait_recv()
    lx_copy(2, xf, xf).wait_recv()
    lc_copy(c).start()
    main_pass(1)
    main_far(0)

    def queries_over_y():
        for i in range(1, NY):
            frm = lax.rem(y + i, NY)
            lq_copy(frm, frm).wait_recv()

    xs = (x, xl, xr, xf)
    def main_queries():
        landed(qs.at[0], s1_recv.at[s_mq])

    several = pairs > 1
    plan = [
        (1, left_slot + c, [queries_over_y]),
        (1, left_slot + 1 - c, [lambda: main_own(2)] * several + [lambda: lc_copy(1 - c).wait_recv()]),
        (0, x * pairs, [lambda: main_far(1), send_partial, main_queries, lambda: main_across(0, 0)]),
        (0, xl * pairs, [lambda: main_own(3), lambda: main_pass(2)] * several + [lambda: main_across(0, 1)]),
        (0, xr * pairs, [lambda: main_far(2)] * several + [lambda: main_across(0, 2)]),
        (0, xf * pairs, [lambda: main_pass(3)] * several + [merge_left] * (not several)
         + [lambda: main_across(0, 3)]),
    ]
    if several:
        plan += [
            (0, x * pairs + 1, [lambda: main_across(1, 0)]),
            (0, xl * pairs + 1, [lambda: main_far(3), merge_left, lambda: main_across(1, 1)]),
            (0, xr * pairs + 1, [lambda: main_across(1, 2)]),
            (0, xf * pairs + 1, [lambda: main_across(1, 3)]),
        ]

    def run_all(events):
        for event in events:
            event()

    def chosen(t, values):
        out = values[0]
        for i in range(1, len(values)):
            out = jnp.where(t == i, values[i], out)
        return out

    def step(t, _):
        for i, (head, slot, first) in enumerate(plan[:-1]):
            pl.when(t == i)(functools.partial(run_all, first))
        attend(chosen(t, [p[0] for p in plan[:-1]]), chosen(t, [p[1] for p in plan[:-1]]))
        return 0

    lax.fori_loop(0, len(plan) - 1, step, 0)

    def send_out(p):
        remote(out_main.at[p], columns(att_ref, me), om_send, om_recv, dev_p(p)).start()

    run_all(plan[-1][2])
    parts = min(4, NZ)
    each = NZ // parts
    turn = [d % NZ for d in ((4, 3, 5, 2, 6, 1, 7, 0) if NZ == 8 else (1, 0))]

    def last(j, _):
        planes = [lax.rem(z + chosen(j, turn[i::each]), NZ) for i in range(each)]
        for plane in planes:
            at, now, total, weight = update(0, plan[-1][1], plane)
            out_main[pl.ds(plane * NY, NY)] = (total / weight).astype(jnp.bfloat16).reshape(NY, TOK, D)
        for plane in planes:
            for i in range(NY):
                p = plane * NY + lax.rem(y + i, NY)
                if i > 0:
                    send_out(p)
                else:
                    @pl.when(p == me)
                    def _():
                        pltpu.make_async_copy(out_main.at[me], columns(att_ref, me), om_recv).start()

                    @pl.when(p != me)
                    def _():
                        send_out(p)
        return 0

    lax.fori_loop(0, parts, last, 0)

    pair_y = y // 2
    for yy in range(NY):
        @pl.when(jnp.logical_not((pair_y == zh) & (yy == y)))
        def _():
            remote(out_left.at[pl.ds(0, ZL)], got_left.at[yy], lo_send.at[0], lo_recv.at[yy],
                   dev(x, c, pair_y * ZL + zl, yy)).wait_recv()
    block_rows = ZL * NY * TOK
    mine = counts_ref[u]
    first = jnp.where(lax.rem(u, 2) == 1, counts_ref[u - lax.rem(u, 2)], 0)
    col = lax.broadcasted_iota(jnp.int32, (MOST, block_rows), 1)
    row = lax.broadcasted_iota(jnp.int32, (MOST, block_rows), 0)
    piece = col // TOK
    place = (lax.rem(piece, ZL) * NY + piece // ZL) * TOK + lax.rem(col, TOK)
    pick = (place == row + first) & (row < mine)
    pick = jnp.where(pick, 1.0, 0.0).astype(jnp.bfloat16)
    left_ref[...] = jnp.dot(pick, got_left[...].reshape(block_rows, D),
                            preferred_element_type=jnp.float32).astype(jnp.bfloat16)

    for n in (0, 0, 1):
        landed(qs.at[0, pl.ds(0, NZ - 1)], s1_send.at[n])
    for n in (2, 3, 4):
        landed(qs.at[0, pl.ds(0, NP - 1)], s1_send.at[n])
    for k in range(chunks):
        m_copy(k, 0, x, xr).wait_send()
        m_copy(k, 1, x, xl).wait_send()
        if k in direct:
            m_copy(k, 4, x, xf).wait_send()
        else:
            m_copy(k, 2, xl, xr).wait_send()
            m_copy(k, 3, xr, xl).wait_send()
        for i in range(4):
            mc_copy(k, i, c, xs[i]).wait_send()
    lx_copy(0, x, xr).wait_send()
    lx_copy(1, x, xl).wait_send()
    lx_copy(2, x, xf).wait_send()
    lc_copy(c).wait_send()
    for i in range(1, NY):
        to = lax.rem(y + i, NY)
        lq_copy(y, to).wait_send()
        for copy in lp_copies(y, to):
            copy.wait_send()
    for zz in range(ZH):
        for k in range(2):
            @pl.when(jnp.logical_not((zz == zh) & (2 * zh + k == y)))
            def _():
                lo_copy(zz, k).wait_send()
    landed(qs.at[0], om_recv)
    landed(qs.at[0, pl.ds(0, NP - 1)], om_send)


def per_device(queries, keys, values, row_counts):
    vmem = pl.BlockSpec(memory_space=pltpu.VMEM)
    hbm = pl.BlockSpec(memory_space=pltpu.HBM)
    order, parts_of, pairs = layout()
    chunks = len(parts_of)
    slots = NX * pairs + 2
    rows = NP * TOK
    group = NZ * TOK
    dma = pltpu.SemaphoreType.DMA
    bf, f32 = jnp.bfloat16, jnp.float32
    flops = 4 * rows * slots * rows * D
    return pl.pallas_call(
        kernel,
        out_shape=(
            jax.ShapeDtypeStruct((TOK, NP * D), bf),
            jax.ShapeDtypeStruct((MOST, D), bf),
        ),
        in_specs=[pl.BlockSpec(memory_space=pltpu.SMEM), hbm, hbm, hbm],
        out_specs=(hbm, vmem),
        scratch_shapes=[
            pltpu.VMEM((slots, NX * NZ, 2 * TOK, D), bf),
            pltpu.VMEM((2, NP, TOK, D), bf),
            pltpu.VMEM((2 * rows, 2 * D), f32),
            pltpu.VMEM((2 * rows, D), f32),
            pltpu.VMEM((NP, TOK, D), bf),
            pltpu.VMEM((rows, D), bf),
            pltpu.VMEM((rows, D), f32),
            pltpu.VMEM((NY, group, D), bf),
            pltpu.VMEM((NY, group, D), f32),
            pltpu.VMEM((NZ, TOK, D), bf),
            pltpu.VMEM((NY, ZL, TOK, D), bf),
            dma((5,)), dma((chunks + 3,)), dma((chunks, 5)), dma((chunks, 5)), dma((chunks, 4)), dma((chunks, 4)),
            dma((3,)), dma((3,)), dma, dma,
            dma((NY,)), dma((NY,)), dma((2, NY)), dma((2, NY)), dma((2 * ZH,)), dma((NY,)), dma, dma, pltpu.SemaphoreType.REGULAR,
        ],
        compiler_params=pltpu.CompilerParams(
            collective_id=0, has_side_effects=True, vmem_limit_bytes=VMEM_LIMIT
        ),
        cost_estimate=pl.CostEstimate(flops=flops, bytes_accessed=2 ** 22, transcendentals=flops // 512),
    )(row_counts, queries, keys, values)


def solution(mesh):
    placed = (P(("blk", "uly"), None), P(("blk", "uly"), None), P(("blk", "uly"), None), P())
    return jax.shard_map(
        per_device,
        mesh=mesh,
        in_specs=placed,
        out_specs=(P(("blk", "uly"), None), P(("blk", "uly"), None)),
        check_vma=False,
    )
```
